256 devices in a mesh: dp: 32 (over x, y, core), tensor: 8 (over z).
Axes of the slice: x: 4, y: 4, z: 8, core: 2. Of those that a mesh axis runs over, the one named last changes fastest.
Arguments:
- activations: bfloat16 [24576, 16384], P('dp', 'tensor'), may hold values from -6 to 6
- cotangent: bfloat16 [24576, 2048], P('dp', 'tensor'), may hold values from -0.59765625 to 0.59765625
- master: float32 [16384, 2048], P('dp', 'tensor')
- moment_one: float32 [16384, 2048], P('dp', 'tensor'), may hold values from -6 to 6
- moment_two: float32 [16384, 2048], P('dp', 'tensor'), may hold values from 0.25 to 4
- writer_of: int32 [16384], replicated, may hold values from 0 to 31, as said below
- previous: float32 [32768, 2048], P('dp', 'tensor'), as said below
Outputs:
- checkpoint_delta: float32 [32768, 2048], P('dp', 'tensor')
- delta_high: bfloat16 [32768, 2048], P('dp', 'tensor')
- moment_one_out: float32 [32768, 2048], P('dp', 'tensor')
- moment_two_out: float32 [32768, 2048], P('dp', 'tensor')
The draws below stay inside these ranges and needn't reach their ends.
Inputs may be any that keep to these rules, and one draw needn't show every extreme that they name: `writer_of`: within each aligned block of 512 rows (the rows of one owner) no writer is named more than 32 times, so no writer is named by more than 1024 rows; in every draw one writer is named exactly 32 times in every block and so by exactly 1024 rows. Rows of previous that some slot names lie within 0.3 of the master row that goes there.
All inputs are finite; a program needn't handle non-finite values.
Results may differ from the reference program's by a relative error of at most 0.001.
Values may be sent and summed in bfloat16 or wider, within the bound.
A program may use at most 128 MiB of HBM per device.

```python
import math
import jax
import jax.numpy as jnp
from jax import lax

D = 16384
KV = 2048
TOKENS = 24576
ROW_DEV = 512
PAIR = 32
CAP = 1024
N_DP = 32


def route_rows(key):
    key = jax.random.fold_in(key, 17)
    owners = D // ROW_DEV
    hottest = jax.random.randint(jax.random.fold_in(key, 1), (), 0, owners).astype(jnp.int32)
    others = (hottest + 1 + jnp.arange(owners - 1, dtype=jnp.int32)) % owners
    reservoir = jnp.repeat(others, PAIR, total_repeat_length=(owners - 1) * PAIR)

    def one_block(block_key):
        shuffled = jax.random.permutation(jax.random.fold_in(block_key, 0), reservoir)
        labels = jnp.concatenate([jnp.full((PAIR,), hottest, jnp.int32), shuffled[:ROW_DEV - PAIR]])
        return jax.random.permutation(jax.random.fold_in(block_key, 1), labels)
    block_keys = jax.random.split(jax.random.fold_in(key, 2), owners)
    return jax.vmap(one_block)(block_keys).reshape(D).astype(jnp.int32)


def base_rows(key):
    return jax.random.normal(jax.random.fold_in(key, 23), (D, KV), jnp.float32)


def draw_writer_of(key, part):
    return route_rows(key)


def draw_master(key, part):
    base = base_rows(key)
    return base


def draw_previous(key, part):
    writers = route_rows(key)
    base = base_rows(key)
    key = jax.random.fold_in(key, 7)
    owners = D // ROW_DEV
    noise = jax.random.normal(key, (owners * CAP, KV), jnp.float32)
    onehot = (writers[:, None] == jnp.arange(owners, dtype=jnp.int32)[None, :]).astype(jnp.int32)
    running = jnp.cumsum(onehot, axis=0).astype(jnp.int32) - onehot
    positions = (writers * CAP + jnp.sum(running * onehot, axis=1)).astype(jnp.int32)
    nearby = base + 0.03 * noise[positions]
    return noise.at[positions].set(nearby)


def raised(values, stream_key, source, target, blocks, factor):
    def block_of(position):
        return (jnp.arange(values.shape[position]) // (values.shape[position] // blocks)).reshape((-1,) + (1,) * (values.ndim - 1 - position))

    first = jax.random.permutation(stream_key, blocks)[block_of(target)]
    other_side = (block_of(target) + blocks // 2) % blocks
    return jnp.where((block_of(source) == first) | (block_of(source) == other_side), factor * values, values)


def steps_of(key, dims, cuts, low, high):
    gain, own = 1.0, jax.random.fold_in(key, 6)
    for position, shards_of in cuts:
        steps = jnp.exp(jax.random.uniform(jax.random.fold_in(own, position), (shards_of,), jnp.float32, low / len(cuts), high / len(cuts)))
        gain = gain * jnp.repeat(steps, dims[position] // shards_of).reshape([-1 if axis == position else 1 for axis in range(len(dims))])
    return gain


def scatter_about(stream_key, shape, width, most, pieces=(), held_as=jnp.bfloat16):
    array = width * jax.random.normal(stream_key, shape, jnp.float32)
    if pieces:
        array = array * steps_of(stream_key, shape, pieces, -0.22, 0.18)
    return jnp.clip(array, -most, most).astype(held_as)


def bell_draw_with(rng, extent, deviation, bound, pieces, heavy, held_as=jnp.bfloat16):
    result = deviation * jax.random.normal(rng, extent, jnp.float32)
    if pieces:
        result = result * steps_of(rng, extent, pieces, -0.22, 0.18)
    return jnp.clip(raised(result, jax.random.fold_in(rng, 3), *heavy), -bound, bound).astype(held_as)


def setup_inputs(seed: int = 0) -> dict:
    splits = jax.random.split(jax.random.key(seed), 8)
    return {
        "activations": bell_draw_with(splits[0], (TOKENS, D), 1.0, 6.0, ((0, 32), (1, 8)), (0, 1, 32, 2.75)),
        "cotangent": scatter_about(splits[1], (TOKENS, KV), 0.1, 0.59765625, ((0, 32), (1, 8))),
        "master": draw_master(jax.random.fold_in(splits[7], 71), 0),
        "moment_one": scatter_about(splits[3], (D, KV), 1.0, 6.0, ((0, 32), (1, 8)), jnp.float32),
        "moment_two": jnp.clip(jnp.exp(math.log(4.0) - 2.7725887 * jax.random.uniform(splits[4], (D, KV), jnp.float32) ** steps_of(splits[4], (D, KV), ((0, 32), (1, 8)), -0.2, 0.2)), 0.25, 4.0),
        "writer_of": draw_writer_of(jax.random.fold_in(splits[7], 71), 0),
        "previous": draw_previous(jax.random.fold_in(splits[7], 71), 0),
    }


learn_rate = 0.01
beta_one = 0.9
beta_two = 0.95
epsilon = 1e-08
decay_rate = 0.1
bias_one = 1.0 - 0.9 ** 10
bias_two = 1.0 - 0.95 ** 10

def adam_rows(gradient, master, moment_one, moment_two):
    first = beta_one * moment_one + (1.0 - beta_one) * gradient
    second = beta_two * moment_two + (1.0 - beta_two) * gradient * gradient
    step_dir = first / bias_one / (jnp.sqrt(second / bias_two) + epsilon) + decay_rate * master
    return (master - learn_rate * step_dir, first, second)

def slot_positions(writer_of):
    writer_ids = jnp.arange(N_DP, dtype=jnp.int32)
    onehot = (writer_of[:, None] == writer_ids[None, :]).astype(jnp.int32)
    running = jnp.cumsum(onehot, axis=0).astype(jnp.int32) - onehot
    row_rank = lax.optimization_barrier(jnp.sum(running * onehot, axis=1)).astype(jnp.int32)
    return (writer_of * CAP + row_rank).astype(jnp.int32)

def reference(activations, cotangent, master, moment_one, moment_two, writer_of, previous):
    gradient = jnp.dot(activations.astype(jnp.float32).T, cotangent.astype(jnp.float32), precision=lax.Precision.HIGHEST, preferred_element_type=jnp.float32)
    updated, first, second = adam_rows(gradient, master, moment_one, moment_two)
    positions = slot_positions(writer_of)
    total_slots = N_DP * CAP
    filled = jnp.zeros((total_slots,), jnp.float32).at[positions].set(1.0)
    empty = jnp.zeros((total_slots, KV), jnp.float32)
    updated_slots = empty.at[positions].set(updated)
    first_slots = empty.at[positions].set(first)
    second_slots = empty.at[positions].set(second)
    delta_out = jnp.where(filled[:, None] > 0.5, (updated_slots - previous) / learn_rate, 0.0)
    return (delta_out, delta_out.astype(jnp.bfloat16), first_slots, second_slots)
```

```python
import functools

import jax
import jax.numpy as jnp
from jax import lax
from jax.experimental import pallas as pl
from jax.experimental.pallas import tpu as pltpu
from jax.sharding import PartitionSpec as P

learn_rate = 0.01
beta_one = 0.9
beta_two = 0.95
epsilon = 1e-08
decay_rate = 0.1
bias_one = 1.0 - 0.9**10
bias_two = 1.0 - 0.95**10


def adam_rows(gradient, master, moment_one, moment_two):
    first = beta_one * moment_one + (1.0 - beta_one) * gradient
    second = beta_two * moment_two + (1.0 - beta_two) * gradient * gradient
    step_dir = first / bias_one / (jnp.sqrt(second / bias_two) + epsilon) + decay_rate * master
    return (master - learn_rate * step_dir, first, second)


def unpack_kernel(base_ref, received_ref, previous_ref, delta_ref, high_ref, first_ref, second_ref, rows_ref):
    sources, pair, _ = received_ref.shape
    capacity, width = previous_ref.shape
    window = pair + 8
    row = lax.broadcasted_iota(jnp.int32, (window, 3 * width), 0)
    for source in range(sources):
        start = base_ref[source]
        shift = lax.rem(start, 8)
        aligned = pl.multiple_of(start - shift, 8)
        block = jnp.concatenate([received_ref[source], received_ref[source, 0:8]], axis=0)
        block = pltpu.roll(block, shift, 0)
        target = rows_ref.at[pl.ds(aligned, window), :]
        target[...] = jnp.where(row >= shift, block, target[...])
    filled = lax.broadcasted_iota(jnp.int32, (capacity, width), 0) < base_ref[sources]
    delta = jnp.where(filled, (rows_ref[0:capacity, 0:width] - previous_ref[...]) / learn_rate, 0.0)
    delta_ref[...] = delta
    high_ref[...] = delta.astype(jnp.bfloat16)
    first_ref[...] = jnp.where(filled, rows_ref[0:capacity, width : 2 * width], 0.0)
    second_ref[...] = jnp.where(filled, rows_ref[0:capacity, 2 * width : 3 * width], 0.0)


def unpack(base, received, previous):
    capacity, width = previous.shape
    pair = received.shape[1]
    vmem = pl.BlockSpec(memory_space=pltpu.VMEM)
    return pl.pallas_call(
        unpack_kernel,
        out_shape=(
            jax.ShapeDtypeStruct((capacity, width), jnp.float32),
            jax.ShapeDtypeStruct((capacity, width), jnp.bfloat16),
            jax.ShapeDtypeStruct((capacity, width), jnp.float32),
            jax.ShapeDtypeStruct((capacity, width), jnp.float32),
        ),
        in_specs=[pl.BlockSpec(memory_space=pltpu.SMEM), vmem, vmem],
        out_specs=(vmem, vmem, vmem, vmem),
        scratch_shapes=[pltpu.VMEM((capacity + pair + 8, received.shape[2]), jnp.float32)],
        compiler_params=pltpu.CompilerParams(vmem_limit_bytes=48 * 1024 * 1024),
    )(base, received, previous)


def local(activations, cotangent, master, moment_one, moment_two, writer_of, previous):
    owners = lax.axis_size("dp")
    planes = lax.axis_size("tensor")
    index = lax.axis_index("dp")
    row_dev, width = master.shape
    capacity = previous.shape[0]
    pair = capacity // owners
    local_owners = owners // planes

    columns = lax.all_gather(cotangent, "tensor", axis=0)
    partial = jnp.einsum(
        "tor,ctk->ocrk",
        activations.reshape(-1, local_owners, row_dev),
        columns,
        preferred_element_type=jnp.float32,
    )
    piece = lax.psum_scatter(
        partial.reshape(owners * row_dev, width), "dp", scatter_dimension=0, tiled=True
    )
    perm = []
    for i in range(owners):
        for t in range(planes):
            perm.append((i * planes + t, (local_owners * t + i // planes) * planes + i % planes))
    gradient = lax.ppermute(piece, ("dp", "tensor"), perm)

    onehot = (
        writer_of.reshape(owners, row_dev)[:, :, None] == jnp.arange(owners, dtype=jnp.int32)
    ).astype(jnp.float32)
    counts = jnp.sum(onehot, axis=1)
    totals = jnp.cumsum(counts, axis=0)
    base = lax.dynamic_slice_in_dim(totals - counts, index, 1, 1)[:, 0]
    total = lax.dynamic_slice_in_dim(totals[-1], index, 1, 0)
    base = jnp.concatenate([base, total]).astype(jnp.int32)

    mine = lax.dynamic_index_in_dim(onehot, index, 0, keepdims=False)
    below = jnp.tril(jnp.ones((row_dev, row_dev), jnp.float32), -1)
    rank = jnp.sum(jnp.dot(below, mine) * mine, axis=1).astype(jnp.int32)
    local_writers = lax.dynamic_slice_in_dim(writer_of, index * row_dev, row_dev, 0)
    place = local_writers * pair + rank
    pack = (jnp.arange(capacity, dtype=jnp.int32)[:, None] == place[None, :]).astype(jnp.float32)

    rows = jnp.concatenate(adam_rows(gradient, master, moment_one, moment_two), axis=1)
    packed = jnp.dot(pack, rows, precision=lax.Precision.HIGHEST)
    received = lax.all_to_all(
        packed.reshape(owners, pair, 3 * width), "dp", split_axis=0, concat_axis=0, tiled=True
    )
    return unpack(base, received, previous)


def solution(mesh):
    spec = P("dp", "tensor")
    return jax.shard_map(
        local,
        mesh=mesh,
        in_specs=(spec, spec, spec, spec, spec, P(), spec),
        out_specs=(spec, spec, spec, spec),
        check_vma=False,
    )
```

```python
import functools

import jax
import jax.numpy as jnp
from jax import lax
from jax.experimental import pallas as pl
from jax.experimental.pallas import tpu as pltpu
from jax.sharding import PartitionSpec as P

learn_rate = 0.01
beta_one = 0.9
beta_two = 0.95
epsilon = 1e-08
decay_rate = 0.1
bias_one = 1.0 - 0.9**10
bias_two = 1.0 - 0.95**10

MESH = pl.DeviceIdType.MESH
SIDE = 4
CORES = 2
DP = SIDE * SIDE * CORES
PLANES = 8
CHUNKS = 2
SCALE_ROWS = 8
TOP = 14.99
ORDER = ((1, 7), (2, 6), (3, 5))


def adam_rows(gradient, master, moment_one, moment_two):
    first = beta_one * moment_one + (1.0 - beta_one) * gradient
    second = beta_two * moment_two + (1.0 - beta_two) * gradient * gradient
    step_dir = first / bias_one / (jnp.sqrt(second / bias_two) + epsilon) + decay_rate * master
    return (master - learn_rate * step_dir, first, second)


def exponent_of(values):
    most = jnp.max(jnp.abs(values), axis=0, keepdims=True)
    return jnp.ceil(jnp.log2(jnp.maximum(most, 1e-30)))


def encode(values, exponent):
    return jnp.round(values * jnp.exp2(TOP - exponent)).astype(jnp.int32)


def unit_of(exponent):
    return 1.0 / jnp.exp2(TOP - exponent)


def join(high, low):
    return (high << 16) | (low & 0xFFFF)


def high_of(word):
    return word >> 16


def low_of(word):
    return (word << 16) >> 16


def coordinates():
    index = lax.axis_index("dp")
    return index // (SIDE * CORES), (index // CORES) % SIDE, index % CORES, lax.axis_index("tensor")


def shift_of(x, y, core):
    along = x * (1 - core) + y * core
    across = y * (1 - core) + x * core
    side = (along % 2 + core) % 2
    far = side * ((8 - across) - 4 * (1 - jnp.minimum(across, 1)))
    return jnp.where(side == 0, across, far)


def owner_of(x, y, core, plane):
    along = x * (1 - core) + y * core
    source = (plane + PLANES - shift_of(x, y, core)) % PLANES
    return 4 * source + 2 * core + along // 2


def main_kernel(
    act_ref, cot_ref, master_ref, one_ref, two_ref, writer_ref,
    gout_ref, mout_ref, pout_ref, base_ref,
    act_own, act_sib, act_t, cot_all, product, acc, asend, arecv, bsend, brecv, zsend, zrecv, gsend,
    m_in, one_in, two_in, msend, psend, codes,
    local_sem, act_sem, cot_sib_sem, zs_sem, zr_sem, fs_sem, fr_sem, as_sem, ar_sem, bs_sem, br_sem,
    ps_sem, pr_sem, gs_sem, gr_sem, ms_sem, mr_sem, qs_sem, qr_sem,
):
    x, y, core, plane = coordinates()
    me = lax.axis_index("dp")
    tokens, _ = cot_ref.shape
    half = act_own.shape[1]
    rows = master_ref.shape[0]
    words = rows // 2
    along = x * (1 - core) + y * core
    across = y * (1 - core) + x * core
    side = (along % 2 + core) % 2
    shift = shift_of(x, y, core)
    sibling = me + 1 - 2 * core
    up = lax.rem(plane + 1, PLANES)
    down = lax.rem(plane + PLANES - 1, PLANES)
    part = tokens // CHUNKS

    def device(a, b):
        return ((a * (1 - core) + b * core) * SIDE + b * (1 - core) + a * core) * CORES + core

    def remote(src, dst, send, recv, dp, at):
        return pltpu.make_async_remote_copy(
            src_ref=src, dst_ref=dst, send_sem=send, recv_sem=recv, device_id=(dp, at), device_id_type=MESH
        )

    def columns_of(which):
        return pl.ds(pl.multiple_of(which * half, 128), half)

    def own_rows(chunk=None):
        if chunk is None:
            return pl.ds(pl.multiple_of(core * tokens, 128), tokens)
        return pl.ds(pl.multiple_of(core * tokens + chunk * part, 128), part)

    loads = [
        pltpu.make_async_copy(act_ref.at[:, columns_of(core)], act_own, local_sem.at[0]),
        pltpu.make_async_copy(cot_ref, cot_all.at[0, own_rows()], local_sem.at[1]),
        pltpu.make_async_copy(master_ref, m_in, local_sem.at[2]),
        pltpu.make_async_copy(one_ref, one_in, local_sem.at[3]),
        pltpu.make_async_copy(two_ref, two_in, local_sem.at[4]),
    ]
    for load in loads:
        load.start()

    barrier = pltpu.get_barrier_semaphore()

    def greet(r, carry):
        pl.semaphore_signal(barrier, inc=1, device_id=(lax.rem(me + r, DP), plane), device_id_type=MESH)
        return carry

    lax.fori_loop(1, DP, greet, 0)
    for at in (up, down):
        pl.semaphore_signal(barrier, inc=1, device_id=(me, at), device_id_type=MESH)

    @pl.when(shift != 0)
    def _():
        pl.semaphore_signal(
            barrier, inc=1, device_id=(me, lax.rem(plane + PLANES - shift, PLANES)), device_id_type=MESH
        )

    pl.semaphore_wait(barrier, DP + 1 + jnp.minimum(shift, 1))

    def z_copy(slot, chunk, direction):
        target = (slot - direction) % PLANES
        rows_here = pl.ds(pl.multiple_of(core * tokens + chunk * part, 128), part)
        if slot == 0:
            src = cot_ref.at[pl.ds(chunk * part, part)]
        else:
            src = cot_all.at[slot, rows_here]
        sem = (target, chunk)
        return remote(
            src, cot_all.at[target, rows_here], zs_sem.at[sem], zr_sem.at[sem], me, up if direction == 1 else down
        )

    def z_last(chunk):
        rows_here = pl.ds(pl.multiple_of(core * tokens + chunk * part, 128), part)
        return remote(
            cot_all.at[5 - 2 * core, rows_here], cot_all.at[4, rows_here], zs_sem.at[4, chunk], zr_sem.at[4, chunk],
            me, lax.rem(plane + 1 - 2 * core + PLANES, PLANES),
        )

    def f_copy(slot):
        src = cot_ref if slot == 0 else cot_all.at[slot, own_rows()]
        return remote(src, cot_all.at[slot, own_rows()], fs_sem.at[slot], fr_sem.at[slot], sibling, plane)

    def f_wait(slot):
        other = pl.ds(pl.multiple_of((1 - core) * tokens, 128), tokens)
        remote(cot_ref, cot_all.at[slot, other], fs_sem.at[slot], fr_sem.at[slot], sibling, plane).wait_recv()

    act_copy = remote(act_ref.at[:, columns_of(1 - core)], act_sib, act_sem.at[0], act_sem.at[1], sibling, plane)
    act_copy.start()
    f_copy(0).start()
    for chunk in range(CHUNKS):
        z_copy(0, chunk, 1).start()
        z_copy(0, chunk, -1).start()

    def transpose_into(source, offset):
        for j in range(half // 128):
            act_t[j * 128 : (j + 1) * 128, pl.ds(pl.multiple_of(offset, 128), tokens)] = source[
                :, j * 128 : (j + 1) * 128
            ].T

    def place_of(owner, split):
        writers = writer_ref[pl.ds(owner, 1), :]
        mine = lax.broadcasted_iota(jnp.int32, (DP, rows), 0) == writers
        below = lax.broadcasted_iota(jnp.int32, (rows, rows), 0) < lax.broadcasted_iota(jnp.int32, (rows, rows), 1)
        before = jnp.dot(
            mine.astype(jnp.bfloat16), below.astype(jnp.bfloat16), preferred_element_type=jnp.float32
        )
        rank = jnp.sum(jnp.where(mine, before, 0.0), axis=0, keepdims=True).astype(jnp.int32)
        if split:
            return (rank >> 4) * (DP * 16) + writers * 16 + (rank & 15)
        return writers * 32 + rank

    def onehot(place, start, count):
        slot = start + lax.broadcasted_iota(jnp.int32, (count, rows), 0)
        return (slot == place).astype(jnp.bfloat16)

    loads[0].wait()
    transpose_into(act_own, core * tokens)
    for load in loads[2:]:
        load.wait()
    e_one = exponent_of(one_in[...])
    code_one = encode(one_in[...], e_one)
    e_two = exponent_of(two_in[...])
    code_two = encode(two_in[...], e_two)
    for k, code in enumerate((code_one, code_two)):
        codes[:, (2 * k) * 256 : (2 * k + 1) * 256] = (code >> 8).astype(jnp.float32).astype(jnp.bfloat16)
        codes[:, (2 * k + 1) * 256 : (2 * k + 2) * 256] = (code & 255).astype(jnp.float32).astype(jnp.bfloat16)
    rest = m_in[...]
    for k in range(3):
        piece = rest.astype(jnp.bfloat16)
        codes[:, (4 + k) * 256 : (5 + k) * 256] = piece
        rest = rest - piece.astype(jnp.float32)
    place_m = place_of(me, False)
    tile = 256
    scale_rows = jnp.concatenate([e_one.astype(jnp.int32)] * 4 + [e_two.astype(jnp.int32)] * 4, axis=0)
    for j in range(1024 // tile):
        packed = jnp.dot(onehot(place_m, j * tile, tile), codes[...], preferred_element_type=jnp.float32)
        q = [packed[:, k * 256 : (k + 1) * 256] for k in range(7)]
        msend[j * 8 : (j + 1) * 8] = (q[4] + q[5] + q[6]).reshape(8, 32, 256)
        word = join((q[0] * 256.0 + q[1]).astype(jnp.int32), (q[2] * 256.0 + q[3]).astype(jnp.int32))
        psend[j * 8 : (j + 1) * 8, 0:32] = word.reshape(8, 32, 256)
        psend[j * 8 : (j + 1) * 8, 32:40] = jnp.broadcast_to(scale_rows[None], (8, 8, 256))

    def m_copy(r):
        to = lax.rem(me + r, DP)
        return remote(msend.at[to], mout_ref.at[me], ms_sem.at[r], mr_sem.at[r], to, plane)

    def p_copy(r):
        to = lax.rem(me + r, DP)
        return remote(psend.at[to], pout_ref.at[me], qs_sem.at[r], qr_sem.at[r], to, plane)

    def m_start(r, carry):
        m_copy(r).start()
        p_copy(r).start()
        return carry

    lax.fori_loop(1, DP, m_start, 0)
    m_self = pltpu.make_async_copy(msend.at[me], mout_ref.at[me], local_sem.at[5])
    p_self = pltpu.make_async_copy(psend.at[me], pout_ref.at[me], local_sem.at[6])
    m_self.start()
    p_self.start()

    act_copy.wait_recv()
    transpose_into(act_sib, (1 - core) * tokens)

    hits = jnp.sum((writer_ref[...] == me).astype(jnp.float32), axis=1, keepdims=True)
    counts = jnp.broadcast_to(hits, (DP, 128)).astype(jnp.bfloat16)
    lower = lax.broadcasted_iota(jnp.int32, (DP + 8, DP), 0) > lax.broadcasted_iota(jnp.int32, (DP + 8, DP), 1)
    base_ref[...] = jnp.dot(lower.astype(jnp.bfloat16), counts, preferred_element_type=jnp.float32).astype(jnp.int32)

    def a_copy(slot, o, a, pair):
        k = lax.rem(along - a + SIDE, SIDE) - 1
        return remote(
            asend.at[slot, o], arecv.at[pair, k], as_sem.at[slot, o], ar_sem.at[pair, k], device(a, across), plane
        )

    def target_of(slot, o):
        return 2 * o + (((1 if slot >= 4 else 0) + core) % 2)

    def write_code(ref, values):
        exponent = exponent_of(values)
        code = encode(values, exponent)
        ref[0:words] = join(code[0:words], code[words:rows])
        ref[words : words + SCALE_ROWS] = jnp.broadcast_to(exponent.astype(jnp.int32), (SCALE_ROWS, values.shape[1]))

    def add_code(ref, total):
        unit = unit_of(ref[words : words + 1, :].astype(jnp.float32))
        word = ref[0:words]
        total[0:words] += high_of(word).astype(jnp.float32) * unit
        total[words:rows] += low_of(word).astype(jnp.float32) * unit

    def multiply(slot, pair):
        for o in range(2):
            a = target_of(slot, o)
            product[...] = jnp.dot(
                act_t[o * rows : (o + 1) * rows, :], cot_all[slot], preferred_element_type=jnp.float32
            )

            @pl.when(a == along)
            def _():
                acc[pair] = product[...]

            @pl.when(a != along)
            def _():
                write_code(asend.at[slot, o], product[...])
                a_copy(slot, o, a, pair).start()

    def b_copy(pair):
        k = lax.rem(across - pair + SIDE, SIDE) - 1
        return remote(bsend.at[pair], brecv.at[k], bs_sem.at[pair], br_sem.at[k], device(along, pair), plane)

    def reduce(pair):
        for k in range(SIDE - 1):
            source = lax.rem(along + k + 1, SIDE)
            remote(
                asend.at[0, 0], arecv.at[pair, k], as_sem.at[0, 0], ar_sem.at[pair, k], device(source, across), plane
            ).wait_recv()
            add_code(arecv.at[pair, k], acc.at[pair])

        @pl.when(across != pair)
        def _():
            write_code(bsend.at[pair], acc[pair])
            b_copy(pair).start()

    def z_wait(slot, chunk):
        rows_here = pl.ds(pl.multiple_of(core * tokens + chunk * part, 128), part)
        remote(
            cot_ref.at[pl.ds(0, part)], cot_all.at[slot, rows_here], zs_sem.at[slot, chunk], zr_sem.at[slot, chunk],
            me, up,
        ).wait_recv()

    loads[1].wait()
    f_wait(0)
    multiply(0, 0)
    for step, (low, high) in enumerate(ORDER):
        for chunk in range(CHUNKS):
            z_wait(low, chunk)
            z_wait(high, chunk)
            if step < 2:
                z_copy(high, chunk, 1).start()
                z_copy(low, chunk, -1).start()
            else:
                z_last(chunk).start()
        f_copy(low).start()
        f_copy(high).start()
        f_wait(low)
        f_wait(high)
        multiply(low, step + 1)
        multiply(high, step + 1)
        if step >= 1:
            reduce(step)
    for chunk in range(CHUNKS):
        z_wait(4, chunk)
    f_copy(4).start()
    reduce(3)
    f_wait(4)
    multiply(4, 0)
    reduce(0)

    for k in range(SIDE - 1):
        source = lax.rem(across + k + 1, SIDE)
        remote(bsend.at[0], brecv.at[k], bs_sem.at[0], br_sem.at[k], device(along, source), plane).wait_recv()
        add_code(brecv.at[k], acc.at[across])

    write_code(zsend, acc[across])
    to_plane = lax.rem(plane + shift, PLANES)

    @pl.when(shift != 0)
    def _():
        move = remote(zsend, zrecv, ps_sem.at[0], pr_sem.at[0], me, to_plane)
        move.start()
        move.wait_recv()

    @pl.when(shift == 0)
    def _():
        zrecv[...] = zsend[...]

    owner = owner_of(x, y, core, plane)
    place_g = place_of(owner, True)
    exponent = zrecv[words : words + SCALE_ROWS]
    word = zrecv[0:words]
    for k, code in enumerate((high_of(word), low_of(word))):
        codes[k * words : (k + 1) * words, 0:256] = (code >> 8).astype(jnp.float32).astype(jnp.bfloat16)
        codes[k * words : (k + 1) * words, 256:512] = (code & 255).astype(jnp.float32).astype(jnp.bfloat16)
    for j in range(2):
        q = []
        for side_of in range(2):
            packed = jnp.dot(
                onehot(place_g, side_of * 512 + j * 256, 256), codes[:, 0:512], preferred_element_type=jnp.float32
            )
            q.append((packed[:, 0:256] * 256.0 + packed[:, 256:512]).astype(jnp.int32))
        gsend[j * 16 : (j + 1) * 16, 0:16] = join(q[0], q[1]).reshape(16, 16, 256)
        gsend[j * 16 : (j + 1) * 16, 16:24] = jnp.broadcast_to(exponent[None], (16, 8, 256))

    def g_copy(r):
        to = lax.rem(me + r, DP)
        return remote(gsend.at[to], gout_ref.at[owner], gs_sem.at[r], gr_sem.at[r], to, plane)

    def g_start(r, carry):
        g_copy(r).start()
        return carry

    lax.fori_loop(1, DP, g_start, 0)
    g_self = pltpu.make_async_copy(gsend.at[me], gout_ref.at[owner], local_sem.at[7])
    g_self.start()

    act_copy.wait_send()
    for slot in (0, 1, 2, 3, 5, 6, 7):
        for chunk in range(CHUNKS):
            if slot in (0, 1, 2):
                z_copy(slot, chunk, -1).wait_send()
            if slot in (0, 7, 6):
                z_copy(slot, chunk, 1).wait_send()
    for chunk in range(CHUNKS):
        z_last(chunk).wait_send()
    for slot in range(PLANES):
        f_copy(slot).wait_send()
        for o in range(2):
            a = target_of(slot, o)

            @pl.when(a != along)
            def _():
                a_copy(slot, o, a, 0).wait_send()

    for pair in range(SIDE):

        @pl.when(across != pair)
        def _():
            b_copy(pair).wait_send()

    @pl.when(shift != 0)
    def _():
        remote(zsend, zrecv, ps_sem.at[0], pr_sem.at[0], me, to_plane).wait_send()

    m_self.wait()
    p_self.wait()
    g_self.wait()

    def finish(r, carry):
        source = lax.rem(me + DP - r, DP)
        from_owner = owner_of(source // (SIDE * CORES), (source // CORES) % SIDE, source % CORES, plane)
        m_copy(r).wait_send()
        p_copy(r).wait_send()
        g_copy(r).wait_send()
        remote(msend.at[0], mout_ref.at[source], ms_sem.at[r], mr_sem.at[r], source, plane).wait_recv()
        remote(psend.at[0], pout_ref.at[source], qs_sem.at[r], qr_sem.at[r], source, plane).wait_recv()
        remote(gsend.at[0], gout_ref.at[from_owner], gs_sem.at[r], gr_sem.at[r], source, plane).wait_recv()
        return carry

    lax.fori_loop(1, DP, finish, 0)


def main_call(activations, cotangent, master, moment_one, moment_two, writers):
    tokens, features = activations.shape
    rows, width = master.shape
    half = features // CORES
    coded = (rows // 2 + SCALE_ROWS, width)
    any_space = pl.BlockSpec(memory_space=pl.ANY)
    vmem = pl.BlockSpec(memory_space=pltpu.VMEM)
    dma = pltpu.SemaphoreType.DMA
    f32, i32, bf16 = jnp.float32, jnp.int32, jnp.bfloat16
    return pl.pallas_call(
        main_kernel,
        name="reduce_and_regroup",
        out_shape=(
            jax.ShapeDtypeStruct((DP, 24, width), i32),
            jax.ShapeDtypeStruct((DP, 32, width), f32),
            jax.ShapeDtypeStruct((DP, 40, width), i32),
            jax.ShapeDtypeStruct((DP + 8, 128), i32),
        ),
        in_specs=[any_space] * 5 + [vmem],
        out_specs=(any_space, any_space, any_space, vmem),
        scratch_shapes=[
            pltpu.VMEM((tokens, half), bf16),
            pltpu.VMEM((tokens, half), bf16),
            pltpu.VMEM((half, 2 * tokens), bf16),
            pltpu.VMEM((PLANES, 2 * tokens, width), bf16),
            pltpu.VMEM((rows, width), f32),
            pltpu.VMEM((SIDE, rows, width), f32),
            pltpu.VMEM((PLANES, 2) + coded, i32),
            pltpu.VMEM((SIDE, SIDE - 1) + coded, i32),
            pltpu.VMEM((SIDE,) + coded, i32),
            pltpu.VMEM((SIDE - 1,) + coded, i32),
            pltpu.VMEM(coded, i32),
            pltpu.VMEM(coded, i32),
            pltpu.VMEM((DP, 24, width), i32),
            pltpu.VMEM((rows, width), f32),
            pltpu.VMEM((rows, width), f32),
            pltpu.VMEM((rows, width), f32),
            pltpu.VMEM((DP, 32, width), f32),
            pltpu.VMEM((DP, 40, width), i32),
            pltpu.VMEM((rows, 7 * width), bf16),
            dma((8,)),
            dma((2,)),
            dma((1,)),
            dma((PLANES, CHUNKS)),
            dma((PLANES, CHUNKS)),
            dma((PLANES,)),
            dma((PLANES,)),
            dma((PLANES, 2)),
            dma((SIDE, SIDE - 1)),
            dma((SIDE,)),
            dma((SIDE - 1,)),
            dma((1,)),
            dma((1,)),
            dma((DP,)),
            dma((DP,)),
            dma((DP,)),
            dma((DP,)),
            dma((DP,)),
            dma((DP,)),
        ],
        compiler_params=pltpu.CompilerParams(
            collective_id=0, has_side_effects=True, vmem_limit_bytes=56 * 1024 * 1024
        ),
        cost_estimate=pl.CostEstimate(
            flops=4 * tokens * features * width * PLANES // 2, bytes_accessed=8 * 1024 * 1024, transcendentals=0
        ),
    )(activations, cotangent, master, moment_one, moment_two, writers)


def finish_kernel(
    base_ref, gradient_ref, master_ref, moments_ref, previous_ref, delta_ref, high_ref, first_ref, second_ref, rows_ref
):
    capacity, width = previous_ref.shape
    pair = capacity // DP
    window = pair + 8
    row = lax.broadcasted_iota(jnp.int32, (window, 3 * width), 0)
    for source in range(DP):
        unit = unit_of(gradient_ref[source, 16:17, :].astype(jnp.float32))
        word = gradient_ref[source, 0:16, :]
        gradient = (
            jnp.concatenate([high_of(word), low_of(word)], axis=0).astype(jnp.float32) * unit
        )
        word = moments_ref[source, 0:32, :]
        one = high_of(word).astype(jnp.float32) * unit_of(moments_ref[source, 32:33, :].astype(jnp.float32))
        two = low_of(word).astype(jnp.float32) * unit_of(moments_ref[source, 36:37, :].astype(jnp.float32))
        block = jnp.concatenate(adam_rows(gradient, master_ref[source], one, two), axis=1)
        start = base_ref[source, 0]
        offset = lax.rem(start, 8)
        aligned = pl.multiple_of(start - offset, 8)
        block = pltpu.roll(jnp.concatenate([block, block[0:8]], axis=0), offset, 0)
        target = rows_ref.at[pl.ds(aligned, window), :]
        target[...] = jnp.where(row >= offset, block, target[...])
    filled = lax.broadcasted_iota(jnp.int32, (capacity, width), 0) < base_ref[DP, 0]
    delta = jnp.where(filled, (rows_ref[0:capacity, 0:width] - previous_ref[...]) / learn_rate, 0.0)
    delta_ref[...] = delta
    high_ref[...] = delta.astype(jnp.bfloat16)
    first_ref[...] = jnp.where(filled, rows_ref[0:capacity, width : 2 * width], 0.0)
    second_ref[...] = jnp.where(filled, rows_ref[0:capacity, 2 * width : 3 * width], 0.0)


def finish_call(base, gradient, master, moments, previous):
    capacity, width = previous.shape
    vmem = pl.BlockSpec(memory_space=pltpu.VMEM)
    return pl.pallas_call(
        finish_kernel,
        name="update_and_place",
        out_shape=(
            jax.ShapeDtypeStruct((capacity, width), jnp.float32),
            jax.ShapeDtypeStruct((capacity, width), jnp.bfloat16),
            jax.ShapeDtypeStruct((capacity, width), jnp.float32),
            jax.ShapeDtypeStruct((capacity, width), jnp.float32),
        ),
        in_specs=[pl.BlockSpec(memory_space=pltpu.SMEM), vmem, vmem, vmem, vmem],
        out_specs=(vmem, vmem, vmem, vmem),
        scratch_shapes=[pltpu.VMEM((capacity + capacity // DP + 8, 3 * width), jnp.float32)],
        compiler_params=pltpu.CompilerParams(vmem_limit_bytes=48 * 1024 * 1024),
    )(base, gradient, master, moments, previous)


def local(activations, cotangent, master, moment_one, moment_two, writer_of, previous):
    writers = writer_of.reshape(DP, master.shape[0])
    gradient, masters, moments, base = main_call(activations, cotangent, master, moment_one, moment_two, writers)
    return finish_call(base, gradient, masters, moments, previous)


def solution(mesh):
    spec = P("dp", "tensor")
    return jax.shard_map(
        local,
        mesh=mesh,
        in_specs=(spec, spec, spec, spec, spec, P(), spec),
        out_specs=(spec, spec, spec, spec),
        check_vma=False,
    )
```

```python
import functools

import jax
import jax.numpy as jnp
from jax import lax
from jax.experimental import pallas as pl
from jax.experimental.pallas import tpu as pltpu
from jax.sharding import PartitionSpec as P

learn_rate = 0.01
beta_one = 0.9
beta_two = 0.95
epsilon = 1e-08
decay_rate = 0.1
bias_one = 1.0 - 0.9**10
bias_two = 1.0 - 0.95**10

MESH = pl.DeviceIdType.MESH
SIDE = 4
CORES = 2
DP = SIDE * SIDE * CORES
PLANES = 8
CHUNKS = 4
SCALE_ROWS = 8
TOP = 14.99
ORDER = ((0,), (1, 7), (2, 6), (3, 5), (4,))


def adam_rows(gradient, master, moment_one, moment_two):
    first = beta_one * moment_one + (1.0 - beta_one) * gradient
    second = beta_two * moment_two + (1.0 - beta_two) * gradient * gradient
    step_dir = first / bias_one / (jnp.sqrt(second / bias_two) + epsilon) + decay_rate * master
    return (master - learn_rate * step_dir, first, second)


def exponent_of(values):
    most = jnp.max(jnp.abs(values), axis=0, keepdims=True)
    return jnp.ceil(jnp.log2(jnp.maximum(most, 1e-30)))


def encode(values, exponent):
    return jnp.round(values * jnp.exp2(TOP - exponent)).astype(jnp.int32)


def unit_of(exponent):
    return 1.0 / jnp.exp2(TOP - exponent)


def join(high, low):
    return (high << 16) | (low & 0xFFFF)


def high_of(word):
    return word >> 16


def low_of(word):
    return (word << 16) >> 16


def coordinates():
    index = lax.axis_index("dp")
    return index // (SIDE * CORES), (index // CORES) % SIDE, index % CORES, lax.axis_index("tensor")


def axes_of(x, y, core):
    return x * (1 - core) + y * core, y * (1 - core) + x * core


def pair_of(slot):
    return slot if slot < 4 else (8 - slot) % 4


def shifts_of(across):
    return across, 8 - across - 4 * (1 - jnp.minimum(across, 1))


def main_kernel(
    act_ref, cot_ref, master_ref, one_ref, two_ref, writer_ref,
    gout_ref, mout_ref, pout_ref, base_ref,
    act_own, act_sib, act_t, cot_all, product, osend, orecv, nsend, nrecv, bsend, brecv, zsend, zrecv, gsend,
    m_in, one_in, two_in, msend, psend, codes,
    local_sem, act_sem, cot_sib_sem, zs_sem, zr_sem, fs_sem, fr_sem, os_sem, or_sem, ns_sem, nr_sem, bs_sem, br_sem,
    ps_sem, pr_sem, gs_sem, gr_sem, ms_sem, mr_sem, qs_sem, qr_sem,
):
    x, y, core, plane = coordinates()
    me = lax.axis_index("dp")
    tokens, _ = cot_ref.shape
    half = act_own.shape[1]
    rows = master_ref.shape[0]
    words = rows // 2
    along, across = axes_of(x, y, core)
    shifts = shifts_of(across)
    sibling = me + 1 - 2 * core
    up = lax.rem(plane + 1, PLANES)
    down = lax.rem(plane + PLANES - 1, PLANES)
    part = tokens // CHUNKS

    def device(a, b):
        return ((a * (1 - core) + b * core) * SIDE + b * (1 - core) + a * core) * CORES + core

    right = device(lax.rem(along + 1, SIDE), across)
    left = device(lax.rem(along + SIDE - 1, SIDE), across)

    def remote(src, dst, send, recv, dp, at):
        return pltpu.make_async_remote_copy(
            src_ref=src, dst_ref=dst, send_sem=send, recv_sem=recv, device_id=(dp, at), device_id_type=MESH
        )

    def columns_of(which):
        return pl.ds(pl.multiple_of(which * half, 128), half)

    def own_rows(chunk=None):
        if chunk is None:
            return pl.ds(pl.multiple_of(core * tokens, 128), tokens)
        return pl.ds(pl.multiple_of(core * tokens + chunk * part, 64), part)

    loads = [
        pltpu.make_async_copy(act_ref.at[:, columns_of(core)], act_own, local_sem.at[0]),
        pltpu.make_async_copy(cot_ref, cot_all.at[0, own_rows()], local_sem.at[1]),
        pltpu.make_async_copy(master_ref, m_in, local_sem.at[2]),
        pltpu.make_async_copy(one_ref, one_in, local_sem.at[3]),
        pltpu.make_async_copy(two_ref, two_in, local_sem.at[4]),
    ]
    for load in loads:
        load.start()

    barrier = pltpu.get_barrier_semaphore()

    def greet(r, carry):
        pl.semaphore_signal(barrier, inc=1, device_id=(lax.rem(me + r, DP), plane), device_id_type=MESH)
        return carry

    lax.fori_loop(1, DP, greet, 0)
    for at in (up, down):
        pl.semaphore_signal(barrier, inc=1, device_id=(me, at), device_id_type=MESH)

    pl.semaphore_signal(
        barrier, inc=1, device_id=(me, lax.rem(plane + PLANES - shifts[1], PLANES)), device_id_type=MESH
    )

    @pl.when(across != 0)
    def _():
        pl.semaphore_signal(
            barrier, inc=1, device_id=(me, lax.rem(plane + PLANES - across, PLANES)), device_id_type=MESH
        )

    pl.semaphore_wait(barrier, DP + 2 + jnp.minimum(across, 1))

    def z_copy(slot, chunk, direction):
        target = (slot - direction) % PLANES
        rows_here = pl.ds(pl.multiple_of(core * tokens + chunk * part, 64), part)
        if slot == 0:
            src = cot_ref.at[pl.ds(chunk * part, part)]
        else:
            src = cot_all.at[slot, rows_here]
        sem = (target, chunk)
        return remote(
            src, cot_all.at[target, rows_here], zs_sem.at[sem], zr_sem.at[sem], me, up if direction == 1 else down
        )

    def z_last(chunk):
        rows_here = pl.ds(pl.multiple_of(core * tokens + chunk * part, 64), part)
        return remote(
            cot_all.at[5 - 2 * core, rows_here], cot_all.at[4, rows_here], zs_sem.at[4, chunk], zr_sem.at[4, chunk],
            me, lax.rem(plane + 1 - 2 * core + PLANES, PLANES),
        )

    def f_copy(slot, chunk):
        rows_here = own_rows(chunk)
        src = cot_ref.at[pl.ds(chunk * part, part)] if slot == 0 else cot_all.at[slot, rows_here]
        sem = (slot, chunk)
        return remote(src, cot_all.at[slot, rows_here], fs_sem.at[sem], fr_sem.at[sem], sibling, plane)

    def f_wait(slot):
        for chunk in range(CHUNKS):
            other = pl.ds(pl.multiple_of((1 - core) * tokens + chunk * part, 64), part)
            sem = (slot, chunk)
            remote(
                cot_ref.at[pl.ds(0, part)], cot_all.at[slot, other], fs_sem.at[sem], fr_sem.at[sem], sibling, plane
            ).wait_recv()

    act_copy = remote(act_ref.at[:, columns_of(1 - core)], act_sib, act_sem.at[0], act_sem.at[1], sibling, plane)
    for chunk in range(CHUNKS):
        z_copy(0, chunk, 1).start()
        z_copy(0, chunk, -1).start()
    act_copy.start()
    for chunk in range(CHUNKS):
        f_copy(0, chunk).start()

    def z_wait(slot, chunk):
        rows_here = pl.ds(pl.multiple_of(core * tokens + chunk * part, 64), part)
        remote(
            cot_ref.at[pl.ds(0, part)], cot_all.at[slot, rows_here], zs_sem.at[slot, chunk], zr_sem.at[slot, chunk],
            me, up,
        ).wait_recv()

    def service(step, chunk):
        for slot in ORDER[step]:
            z_wait(slot, chunk)
        if step < 3:
            z_copy(ORDER[step][1], chunk, 1).start()
            z_copy(ORDER[step][0], chunk, -1).start()
        elif step == 3:
            z_last(chunk).start()
        for slot in ORDER[step]:
            f_copy(slot, chunk).start()

    def transpose_into(source, offset):
        for j in range(half // 128):
            act_t[j * 128 : (j + 1) * 128, pl.ds(pl.multiple_of(offset, 128), tokens)] = source[
                :, j * 128 : (j + 1) * 128
            ].T

    def place_of(owner, split):
        writers = writer_ref[pl.ds(owner, 1), :]
        mine = lax.broadcasted_iota(jnp.int32, (DP, rows), 0) == writers
        below = lax.broadcasted_iota(jnp.int32, (rows, rows), 0) < lax.broadcasted_iota(jnp.int32, (rows, rows), 1)
        before = jnp.dot(
            mine.astype(jnp.bfloat16), below.astype(jnp.bfloat16), preferred_element_type=jnp.float32
        )
        rank = jnp.sum(jnp.where(mine, before, 0.0), axis=0, keepdims=True).astype(jnp.int32)
        if split:
            return (rank >> 4) * (DP * 16) + writers * 16 + (rank & 15)
        return writers * 32 + rank

    def onehot(place, start, count):
        slot = start + lax.broadcasted_iota(jnp.int32, (count, rows), 0)
        return (slot == place).astype(jnp.bfloat16)

    loads[0].wait()
    transpose_into(act_own, core * tokens)
    for load in loads[2:]:
        load.wait()
    e_one = exponent_of(one_in[...])
    code_one = encode(one_in[...], e_one)
    e_two = exponent_of(two_in[...])
    code_two = encode(two_in[...], e_two)
    for k, code in enumerate((code_one, code_two)):
        codes[:, (2 * k) * 256 : (2 * k + 1) * 256] = (code >> 8).astype(jnp.float32).astype(jnp.bfloat16)
        codes[:, (2 * k + 1) * 256 : (2 * k + 2) * 256] = (code & 255).astype(jnp.float32).astype(jnp.bfloat16)
    rest = m_in[...]
    for k in range(3):
        piece = rest.astype(jnp.bfloat16)
        codes[:, (4 + k) * 256 : (5 + k) * 256] = piece
        rest = rest - piece.astype(jnp.float32)
    place_m = place_of(me, False)
    tile = 256
    scale_rows = jnp.concatenate([e_one.astype(jnp.int32)] * 4 + [e_two.astype(jnp.int32)] * 4, axis=0)
    for j in range(1024 // tile):
        packed = jnp.dot(onehot(place_m, j * tile, tile), codes[...], preferred_element_type=jnp.float32)
        q = [packed[:, k * 256 : (k + 1) * 256] for k in range(7)]
        msend[j * 8 : (j + 1) * 8] = (q[4] + q[5] + q[6]).reshape(8, 32, 256)
        word = join((q[0] * 256.0 + q[1]).astype(jnp.int32), (q[2] * 256.0 + q[3]).astype(jnp.int32))
        psend[j * 8 : (j + 1) * 8, 0:32] = word.reshape(8, 32, 256)
        psend[j * 8 : (j + 1) * 8, 32:40] = jnp.broadcast_to(scale_rows[None], (8, 8, 256))

    def m_copy(r):
        to = lax.rem(me + r, DP)
        return remote(msend.at[to], mout_ref.at[me], ms_sem.at[r], mr_sem.at[r], to, plane)

    def p_copy(r):
        to = lax.rem(me + r, DP)
        return remote(psend.at[to], pout_ref.at[me], qs_sem.at[r], qr_sem.at[r], to, plane)

    def m_start(r, carry):
        m_copy(r).start()
        return carry

    lax.fori_loop(1, DP, m_start, 0)
    m_self = pltpu.make_async_copy(msend.at[me], mout_ref.at[me], local_sem.at[5])
    p_self = pltpu.make_async_copy(psend.at[me], pout_ref.at[me], local_sem.at[6])
    m_self.start()
    p_self.start()

    service(1, 0)
    act_copy.wait_recv()
    transpose_into(act_sib, (1 - core) * tokens)

    hits = jnp.sum((writer_ref[...] == me).astype(jnp.float32), axis=1, keepdims=True)
    counts = jnp.broadcast_to(hits, (DP, 128)).astype(jnp.bfloat16)
    lower = lax.broadcasted_iota(jnp.int32, (DP + 8, DP), 0) > lax.broadcasted_iota(jnp.int32, (DP + 8, DP), 1)
    base_ref[...] = jnp.dot(lower.astype(jnp.bfloat16), counts, preferred_element_type=jnp.float32).astype(jnp.int32)

    def write_code(values, *refs):
        exponent = exponent_of(values)
        code = encode(values, exponent)
        word = join(code[0:words], code[words:rows])
        count = words // len(refs)
        for i, ref in enumerate(refs):
            ref[0:count] = word[i * count : (i + 1) * count]
            ref[count : count + SCALE_ROWS] = jnp.broadcast_to(
                exponent.astype(jnp.int32), (SCALE_ROWS, values.shape[1])
            )

    def add_code(ref, total, start, count):
        unit = unit_of(ref[count : count + 1, :].astype(jnp.float32))
        word = ref[0:count]
        total[start : start + count] += high_of(word).astype(jnp.float32) * unit
        total[words + start : words + start + count] += low_of(word).astype(jnp.float32) * unit

    def far_copy(slot, i):
        return remote(
            osend.at[slot, i], orecv.at[slot, i], os_sem.at[slot, i], or_sem.at[slot, i], left if i else right, plane
        )

    def near_copy(slot, i):
        return remote(
            nsend.at[slot, i], nrecv.at[slot, i], ns_sem.at[slot, i], nr_sem.at[slot, i], left if i else right, plane
        )

    def b_copy(slot):
        k = lax.rem(across - pair_of(slot) + SIDE, SIDE) - 1
        j = 0 if slot < 4 else 1
        return remote(
            bsend.at[slot], brecv.at[j, k], bs_sem.at[slot], br_sem.at[j, k], device(along, pair_of(slot)), plane
        )

    def multiply(slot):
        for o in range(2):
            block = jnp.dot(
                act_t[o * rows : (o + 1) * rows, :], cot_all[slot], preferred_element_type=jnp.float32
            )
            product[slot, 2 * o] = block[:, 0:128]
            product[slot, 2 * o + 1] = block[:, 128:256]
        write_code(product[slot, lax.rem(along + 2, SIDE)], osend.at[slot, 0], osend.at[slot, 1])
        far_copy(slot, 0).start()
        far_copy(slot, 1).start()

    def pass_on(slot):
        for i, turn in ((0, 1), (1, SIDE - 1)):
            target = lax.rem(along + turn, SIDE)
            far_copy(slot, i).wait_recv()
            add_code(orecv.at[slot, i], product.at[slot, target], i * (words // 2), words // 2)
            write_code(product[slot, target], nsend.at[slot, i])
            near_copy(slot, i).start()

    def reduce(slot):
        for i in range(2):
            near_copy(slot, i).wait_recv()
            add_code(nrecv.at[slot, i], product.at[slot, along], 0, words)

        @pl.when(across != pair_of(slot))
        def _():
            write_code(product[slot, along], bsend.at[slot])
            b_copy(slot).start()

    def p_move(j):
        return remote(
            zsend.at[j], zrecv.at[j], ps_sem.at[j], pr_sem.at[j], me, lax.rem(plane + shifts[j], PLANES)
        )

    def whole(j):
        slot = shifts[j]
        for k in range(SIDE - 1):
            source = lax.rem(across + k + 1, SIDE)
            remote(
                bsend.at[0], brecv.at[j, k], bs_sem.at[0], br_sem.at[j, k], device(along, source), plane
            ).wait_recv()
            add_code(brecv.at[j, k], product.at[slot, along], 0, words)
        write_code(product[slot, along], zsend.at[j])

    loads[1].wait()
    f_wait(0)
    multiply(0)
    for chunk in range(1, CHUNKS):
        service(1, chunk)
    for step in (1, 2, 3):
        f_wait(ORDER[step][0])
        multiply(ORDER[step][0])
        service(step + 1, 0)
        f_wait(ORDER[step][1])
        multiply(ORDER[step][1])
        service(step + 1, 1)
        for slot in ORDER[step - 1]:
            pass_on(slot)
        service(step + 1, 2)
        if step >= 2:
            for slot in ORDER[step - 2]:
                reduce(slot)
        service(step + 1, 3)
    f_wait(4)
    multiply(4)
    for slot in ORDER[3]:
        pass_on(slot)
    for slot in ORDER[2]:
        reduce(slot)
    pass_on(4)
    for slot in ORDER[3] + ORDER[4]:
        reduce(slot)

    def p_start(r, carry):
        p_copy(r).start()
        return carry

    lax.fori_loop(1, DP, p_start, 0)

    whole(0)

    @pl.when(across != 0)
    def _():
        p_move(0).start()

    whole(1)
    p_move(1).start()

    owners = [4 * lax.rem(plane + PLANES - shift, PLANES) + 2 * core + along // 2 for shift in shifts]
    for j in range(2):
        place_g = place_of(owners[j], True)
        if j == 0:

            @pl.when(across != 0)
            def _():
                p_move(0).wait_recv()

            @pl.when(across == 0)
            def _():
                zrecv[0] = zsend[0]

        else:
            p_move(1).wait_recv()
        exponent = zrecv[j, words : words + SCALE_ROWS]
        word = zrecv[j, 0:words]
        for k, code in enumerate((high_of(word), low_of(word))):
            codes[k * words : (k + 1) * words, 0:128] = (code >> 8).astype(jnp.float32).astype(jnp.bfloat16)
            codes[k * words : (k + 1) * words, 128:256] = (code & 255).astype(jnp.float32).astype(jnp.bfloat16)
        for i in range(2):
            q = []
            for side_of in range(2):
                packed = jnp.dot(
                    onehot(place_g, side_of * 512 + i * 256, 256), codes[:, 0:256], preferred_element_type=jnp.float32
                )
                q.append((packed[:, 0:128] * 256.0 + packed[:, 128:256]).astype(jnp.int32))
            gsend[i * 16 : (i + 1) * 16, j, 0:16] = join(q[0], q[1]).reshape(16, 16, 128)
            gsend[i * 16 : (i + 1) * 16, j, 16:24] = jnp.broadcast_to(exponent[None], (16, 8, 128))

    def g_copy(r):
        to = lax.rem(me + r, DP)
        return remote(gsend.at[to], gout_ref.at[me], gs_sem.at[r], gr_sem.at[r], to, plane)

    def g_start(r, carry):
        g_copy(r).start()
        return carry

    lax.fori_loop(1, DP, g_start, 0)
    g_self = pltpu.make_async_copy(gsend.at[me], gout_ref.at[me], local_sem.at[7])
    g_self.start()

    act_copy.wait_send()
    for slot in (0, 1, 2, 3, 5, 6, 7):
        for chunk in range(CHUNKS):
            if slot in (0, 1, 2):
                z_copy(slot, chunk, -1).wait_send()
            if slot in (0, 7, 6):
                z_copy(slot, chunk, 1).wait_send()
    for chunk in range(CHUNKS):
        z_last(chunk).wait_send()
    for slot in range(PLANES):
        for chunk in range(CHUNKS):
            f_copy(slot, chunk).wait_send()
        for i in range(2):
            far_copy(slot, i).wait_send()
            near_copy(slot, i).wait_send()

        @pl.when(across != pair_of(slot))
        def _():
            b_copy(slot).wait_send()

    @pl.when(across != 0)
    def _():
        p_move(0).wait_send()

    p_move(1).wait_send()
    m_self.wait()
    p_self.wait()
    g_self.wait()

    def finish(r, carry):
        source = lax.rem(me + DP - r, DP)
        m_copy(r).wait_send()
        p_copy(r).wait_send()
        g_copy(r).wait_send()
        remote(msend.at[0], mout_ref.at[source], ms_sem.at[r], mr_sem.at[r], source, plane).wait_recv()
        remote(psend.at[0], pout_ref.at[source], qs_sem.at[r], qr_sem.at[r], source, plane).wait_recv()
        remote(gsend.at[0], gout_ref.at[source], gs_sem.at[r], gr_sem.at[r], source, plane).wait_recv()
        return carry

    lax.fori_loop(1, DP, finish, 0)


def main_call(activations, cotangent, master, moment_one, moment_two, writers):
    tokens, features = activations.shape
    rows, width = master.shape
    half = features // CORES
    side = width // 2
    coded = (rows // 2 + SCALE_ROWS, side)
    any_space = pl.BlockSpec(memory_space=pl.ANY)
    vmem = pl.BlockSpec(memory_space=pltpu.VMEM)
    dma = pltpu.SemaphoreType.DMA
    f32, i32, bf16 = jnp.float32, jnp.int32, jnp.bfloat16
    return pl.pallas_call(
        main_kernel,
        name="reduce_and_regroup",
        out_shape=(
            jax.ShapeDtypeStruct((DP, 2, 24, side), i32),
            jax.ShapeDtypeStruct((DP, 32, width), f32),
            jax.ShapeDtypeStruct((DP, 40, width), i32),
            jax.ShapeDtypeStruct((DP + 8, 128), i32),
        ),
        in_specs=[any_space] * 5 + [vmem],
        out_specs=(any_space, any_space, any_space, vmem),
        scratch_shapes=[
            pltpu.VMEM((tokens, half), bf16),
            pltpu.VMEM((tokens, half), bf16),
            pltpu.VMEM((half, 2 * tokens), bf16),
            pltpu.VMEM((PLANES, 2 * tokens, width), bf16),
            pltpu.VMEM((PLANES, SIDE, rows, side), f32),
            pltpu.VMEM((PLANES, 2, rows // 4 + SCALE_ROWS, side), i32),
            pltpu.VMEM((PLANES, 2, rows // 4 + SCALE_ROWS, side), i32),
            pltpu.VMEM((PLANES, 2) + coded, i32),
            pltpu.VMEM((PLANES, 2) + coded, i32),
            pltpu.VMEM((PLANES,) + coded, i32),
            pltpu.VMEM((2, SIDE - 1) + coded, i32),
            pltpu.VMEM((2,) + coded, i32),
            pltpu.VMEM((2,) + coded, i32),
            pltpu.VMEM((DP, 2, 24, side), i32),
            pltpu.VMEM((rows, width), f32),
            pltpu.VMEM((rows, width), f32),
            pltpu.VMEM((rows, width), f32),
            pltpu.VMEM((DP, 32, width), f32),
            pltpu.VMEM((DP, 40, width), i32),
            pltpu.VMEM((rows, 7 * width), bf16),
            dma((8,)),
            dma((2,)),
            dma((1,)),
            dma((PLANES, CHUNKS)),
            dma((PLANES, CHUNKS)),
            dma((PLANES, CHUNKS)),
            dma((PLANES, CHUNKS)),
            dma((PLANES, 2)),
            dma((PLANES, 2)),
            dma((PLANES, 2)),
            dma((PLANES, 2)),
            dma((PLANES,)),
            dma((2, SIDE - 1)),
            dma((2,)),
            dma((2,)),
            dma((DP,)),
            dma((DP,)),
            dma((DP,)),
            dma((DP,)),
            dma((DP,)),
            dma((DP,)),
        ],
        compiler_params=pltpu.CompilerParams(
            collective_id=0, has_side_effects=True, vmem_limit_bytes=56 * 1024 * 1024
        ),
        cost_estimate=pl.CostEstimate(
            flops=4 * tokens * features * width * PLANES // 2, bytes_accessed=8 * 1024 * 1024, transcendentals=0
        ),
    )(activations, cotangent, master, moment_one, moment_two, writers)


def source_of(owner, part, plane):
    slot = lax.rem(plane + PLANES - owner // 4, PLANES)
    late = slot // 4
    across = jnp.where(late == 0, slot, lax.rem(PLANES - slot, 4))
    core = (owner // 2) % 2
    x, y = axes_of(2 * (owner % 2) + part, across, core)
    return (x * SIDE + y) * CORES + core, late


def finish_kernel(
    base_ref, gradient_hbm, master_hbm, moments_hbm, previous_hbm,
    delta_ref, high_ref, first_ref, second_ref,
    gradient_ref, master_ref, moments_ref, previous_ref, rows_ref, sem,
):
    loads = [
        pltpu.make_async_copy(moments_hbm, moments_ref, sem.at[0]),
        pltpu.make_async_copy(master_hbm, master_ref, sem.at[1]),
        pltpu.make_async_copy(gradient_hbm, gradient_ref, sem.at[2]),
        pltpu.make_async_copy(previous_hbm, previous_ref, sem.at[3]),
    ]
    for load in loads:
        load.start()
    plane = lax.axis_index("tensor")
    capacity, width = previous_ref.shape
    pair = capacity // DP
    window = pair + 8
    row = lax.broadcasted_iota(jnp.int32, (window, 3 * width), 0)
    for load in loads[:3]:
        load.wait()
    for owner in range(DP):
        parts = []
        for part in range(2):
            source, late = source_of(owner, part, plane)
            unit = unit_of(gradient_ref[source, late, 16:17, :].astype(jnp.float32))
            word = gradient_ref[source, late, 0:16, :]
            parts.append(jnp.concatenate([high_of(word), low_of(word)], axis=0).astype(jnp.float32) * unit)
        gradient = jnp.concatenate(parts, axis=1)
        word = moments_ref[owner, 0:32, :]
        one = high_of(word).astype(jnp.float32) * unit_of(moments_ref[owner, 32:33, :].astype(jnp.float32))
        two = low_of(word).astype(jnp.float32) * unit_of(moments_ref[owner, 36:37, :].astype(jnp.float32))
        block = jnp.concatenate(adam_rows(gradient, master_ref[owner], one, two), axis=1)
        start = base_ref[owner, 0]
        offset = lax.rem(start, 8)
        aligned = pl.multiple_of(start - offset, 8)
        block = pltpu.roll(jnp.concatenate([block, block[0:8]], axis=0), offset, 0)
        target = rows_ref.at[pl.ds(aligned, window), :]
        target[...] = jnp.where(row >= offset, block, target[...])
    loads[3].wait()
    filled = lax.broadcasted_iota(jnp.int32, (capacity, width), 0) < base_ref[DP, 0]
    delta = jnp.where(filled, (rows_ref[0:capacity, 0:width] - previous_ref[...]) / learn_rate, 0.0)
    delta_ref[...] = delta
    high_ref[...] = delta.astype(jnp.bfloat16)
    first_ref[...] = jnp.where(filled, rows_ref[0:capacity, width : 2 * width], 0.0)
    second_ref[...] = jnp.where(filled, rows_ref[0:capacity, 2 * width : 3 * width], 0.0)


def finish_call(base, gradient, master, moments, previous):
    capacity, width = previous.shape
    vmem = pl.BlockSpec(memory_space=pltpu.VMEM)
    any_space = pl.BlockSpec(memory_space=pl.ANY)
    return pl.pallas_call(
        finish_kernel,
        name="update_and_place",
        out_shape=(
            jax.ShapeDtypeStruct((capacity, width), jnp.float32),
            jax.ShapeDtypeStruct((capacity, width), jnp.bfloat16),
            jax.ShapeDtypeStruct((capacity, width), jnp.float32),
            jax.ShapeDtypeStruct((capacity, width), jnp.float32),
        ),
        in_specs=[pl.BlockSpec(memory_space=pltpu.SMEM)] + [any_space] * 4,
        out_specs=(vmem, vmem, vmem, vmem),
        scratch_shapes=[
            pltpu.VMEM(gradient.shape, gradient.dtype),
            pltpu.VMEM(master.shape, master.dtype),
            pltpu.VMEM(moments.shape, moments.dtype),
            pltpu.VMEM(previous.shape, previous.dtype),
            pltpu.VMEM((capacity + capacity // DP + 8, 3 * width), jnp.float32),
            pltpu.SemaphoreType.DMA((4,)),
        ],
        compiler_params=pltpu.CompilerParams(vmem_limit_bytes=60 * 1024 * 1024),
    )(base, gradient, master, moments, previous)


def local(activations, cotangent, master, moment_one, moment_two, writer_of, previous):
    writers = writer_of.reshape(DP, master.shape[0])
    gradient, masters, moments, base = main_call(activations, cotangent, master, moment_one, moment_two, writers)
    return finish_call(base, gradient, masters, moments, previous)


def solution(mesh):
    spec = P("dp", "tensor")
    return jax.shard_map(
        local,
        mesh=mesh,
        in_specs=(spec, spec, spec, spec, spec, P(), spec),
        out_specs=(spec, spec, spec, spec),
        check_vma=False,
    )
```

```python
import functools

import jax
import jax.numpy as jnp
from jax import lax
from jax.experimental import pallas as pl
from jax.experimental.pallas import tpu as pltpu
from jax.sharding import PartitionSpec as P

learn_rate = 0.01
beta_one = 0.9
beta_two = 0.95
epsilon = 1e-08
decay_rate = 0.1
bias_one = 1.0 - 0.9**10
bias_two = 1.0 - 0.95**10

MESH = pl.DeviceIdType.MESH
SIDE = 4
CORES = 2
DP = SIDE * SIDE * CORES
PLANES = 8
CHUNKS = 4
SCALE_ROWS = 8
TOP = 14.99
PERIOD = 0.625
STEP = PERIOD / 2**20
OFFSET = 128
SPREAD = ((1, 4), (4, 7), (7, 10), (10, 13), (13, 15), (15, 17), (17, 19), (19, 21), (21, 22), (22, 23), (23, 23), (23, 23), (23, 23), (23, 23), (23, 23), (23, 23))
ORDER = ((0,), (1, 7), (2, 6), (3, 5), (4,))


def moments_of(gradient, moment_one, moment_two):
    first = beta_one * moment_one + (1.0 - beta_one) * gradient
    second = beta_two * moment_two + (1.0 - beta_two) * gradient * gradient
    return first, second


def step_of(first, second, master):
    return first / bias_one / (jnp.sqrt(second / bias_two) + epsilon) + decay_rate * master


def exponent_of(values):
    most = jnp.max(jnp.abs(values), axis=0, keepdims=True)
    return jnp.ceil(jnp.log2(jnp.maximum(most, 1e-30)))


def encode(values, exponent):
    return jnp.round(values * jnp.exp2(TOP - exponent)).astype(jnp.int32)


def unit_of(exponent):
    return 1.0 / jnp.exp2(TOP - exponent)


def within_period(values):
    return values - jnp.floor(values * (1.0 / PERIOD)) * PERIOD


def join(high, low):
    return (high << 16) | (low & 0xFFFF)


def high_of(word):
    return word >> 16


def low_of(word):
    return (word << 16) >> 16


def coordinates():
    index = lax.axis_index("dp")
    return index // (SIDE * CORES), (index // CORES) % SIDE, index % CORES, lax.axis_index("tensor")


def axes_of(x, y, core):
    return x * (1 - core) + y * core, y * (1 - core) + x * core


def pair_of(slot):
    return slot if slot < 4 else (8 - slot) % 4


def shifts_of(across):
    return across, 8 - across - 4 * (1 - jnp.minimum(across, 1))


def main_kernel(
    act_ref, cot_ref, master_ref, one_ref, two_ref, writer_flat,
    gout_ref, pout_ref, base_ref,
    act_own, act_sib, act_t, cot_all, product, osend, orecv, nsend, nrecv, bsend, brecv, zsend, zrecv, gsend,
    m_in, one_in, two_in, psend, codes, writer_ref,
    local_sem, act_sem, cot_sib_sem, zs_sem, zr_sem, fs_sem, fr_sem, os_sem, or_sem, ns_sem, nr_sem, bs_sem, br_sem,
    ps_sem, pr_sem, gs_sem, gr_sem, qs_sem, qr_sem,
):
    x, y, core, plane = coordinates()
    me = lax.axis_index("dp")
    tokens, _ = cot_ref.shape
    half = act_own.shape[1]
    rows = master_ref.shape[0]
    words = rows // 2
    along, across = axes_of(x, y, core)
    shifts = shifts_of(across)
    sibling = me + 1 - 2 * core
    up = lax.rem(plane + 1, PLANES)
    down = lax.rem(plane + PLANES - 1, PLANES)
    part = tokens // CHUNKS

    def device(a, b):
        return ((a * (1 - core) + b * core) * SIDE + b * (1 - core) + a * core) * CORES + core

    right = device(lax.rem(along + 1, SIDE), across)
    left = device(lax.rem(along + SIDE - 1, SIDE), across)

    def remote(src, dst, send, recv, dp, at):
        return pltpu.make_async_remote_copy(
            src_ref=src, dst_ref=dst, send_sem=send, recv_sem=recv, device_id=(dp, at), device_id_type=MESH
        )

    def columns_of(which):
        return pl.ds(pl.multiple_of(which * half, 128), half)

    def own_rows(chunk=None):
        if chunk is None:
            return pl.ds(pl.multiple_of(core * tokens, 128), tokens)
        return pl.ds(pl.multiple_of(core * tokens + chunk * part, 64), part)

    loads = [
        pltpu.make_async_copy(act_ref.at[:, columns_of(core)], act_own, local_sem.at[0]),
        pltpu.make_async_copy(cot_ref, cot_all.at[0, own_rows()], local_sem.at[1]),
        pltpu.make_async_copy(master_ref, m_in, local_sem.at[2]),
        pltpu.make_async_copy(one_ref, one_in, local_sem.at[3]),
        pltpu.make_async_copy(two_ref, two_in, local_sem.at[4]),
    ]
    for load in loads:
        load.start()

    barrier = pltpu.get_barrier_semaphore()

    def greet(r, carry):
        pl.semaphore_signal(barrier, inc=1, device_id=(lax.rem(me + r, DP), plane), device_id_type=MESH)
        return carry

    lax.fori_loop(1, DP, greet, 0)
    for at in (up, down):
        pl.semaphore_signal(barrier, inc=1, device_id=(me, at), device_id_type=MESH)

    pl.semaphore_signal(
        barrier, inc=1, device_id=(me, lax.rem(plane + PLANES - shifts[1], PLANES)), device_id_type=MESH
    )

    @pl.when(across != 0)
    def _():
        pl.semaphore_signal(
            barrier, inc=1, device_id=(me, lax.rem(plane + PLANES - across, PLANES)), device_id_type=MESH
        )

    def place_of(owner, split):
        writers = writer_ref[pl.ds(owner, 1), :]
        mine = lax.broadcasted_iota(jnp.int32, (DP, rows), 0) == writers
        below = lax.broadcasted_iota(jnp.int32, (rows, rows), 0) < lax.broadcasted_iota(jnp.int32, (rows, rows), 1)
        before = jnp.dot(
            mine.astype(jnp.bfloat16), below.astype(jnp.bfloat16), preferred_element_type=jnp.float32
        )
        rank = jnp.sum(jnp.where(mine, before, 0.0), axis=0, keepdims=True).astype(jnp.int32)
        if split:
            return (rank >> 4) * (DP * 16) + writers * 16 + (rank & 15)
        return writers * 32 + rank

    for k in range(rows // 128):
        writer_ref[:, k * 128 : (k + 1) * 128] = writer_flat[pl.ds(k, DP, stride=rows // 128), :]

    place_m = place_of(me, False)
    pl.semaphore_wait(barrier, DP + 2 + jnp.minimum(across, 1))

    def z_copy(slot, chunk, direction):
        target = (slot - direction) % PLANES
        rows_here = pl.ds(pl.multiple_of(core * tokens + chunk * part, 64), part)
        if slot == 0:
            src = cot_ref.at[pl.ds(chunk * part, part)]
        else:
            src = cot_all.at[slot, rows_here]
        sem = (target, chunk)
        return remote(
            src, cot_all.at[target, rows_here], zs_sem.at[sem], zr_sem.at[sem], me, up if direction == 1 else down
        )

    def z_last(chunk):
        rows_here = pl.ds(pl.multiple_of(core * tokens + chunk * part, 64), part)
        return remote(
            cot_all.at[5 - 2 * core, rows_here], cot_all.at[4, rows_here], zs_sem.at[4, chunk], zr_sem.at[4, chunk],
            me, lax.rem(plane + 1 - 2 * core + PLANES, PLANES),
        )

    def f_copy(slot, chunk):
        rows_here = own_rows(chunk)
        src = cot_ref.at[pl.ds(chunk * part, part)] if slot == 0 else cot_all.at[slot, rows_here]
        sem = (slot, chunk)
        return remote(src, cot_all.at[slot, rows_here], fs_sem.at[sem], fr_sem.at[sem], sibling, plane)

    def f_wait(slot):
        for chunk in range(CHUNKS):
            other = pl.ds(pl.multiple_of((1 - core) * tokens + chunk * part, 64), part)
            sem = (slot, chunk)
            remote(
                cot_ref.at[pl.ds(0, part)], cot_all.at[slot, other], fs_sem.at[sem], fr_sem.at[sem], sibling, plane
            ).wait_recv()

    act_copy = remote(act_ref.at[:, columns_of(1 - core)], act_sib, act_sem.at[0], act_sem.at[1], sibling, plane)
    for chunk in range(CHUNKS):
        z_copy(0, chunk, 1).start()
        z_copy(0, chunk, -1).start()
    act_copy.start()
    for chunk in range(CHUNKS):
        f_copy(0, chunk).start()

    def z_wait(slot, chunk):
        rows_here = pl.ds(pl.multiple_of(core * tokens + chunk * part, 64), part)
        remote(
            cot_ref.at[pl.ds(0, part)], cot_all.at[slot, rows_here], zs_sem.at[slot, chunk], zr_sem.at[slot, chunk],
            me, up,
        ).wait_recv()

    def p_copy(r):
        to = lax.rem(me + r, DP)
        return remote(psend.at[to], pout_ref.at[me], qs_sem.at[r], qr_sem.at[r], to, plane)

    def service(step, chunk):
        for slot in ORDER[step]:
            z_wait(slot, chunk)
        if step < 3:
            z_copy(ORDER[step][1], chunk, 1).start()
            z_copy(ORDER[step][0], chunk, -1).start()
        elif step == 3:
            z_last(chunk).start()
        for slot in ORDER[step]:
            f_copy(slot, chunk).start()
        for r in range(*SPREAD[4 * step - 4 + chunk]):
            p_copy(r).start()

    def transpose_into(source, offset):
        for j in range(half // 128):
            act_t[j * 128 : (j + 1) * 128, pl.ds(pl.multiple_of(offset, 128), tokens)] = source[
                :, j * 128 : (j + 1) * 128
            ].T

    def onehot(place, start, count):
        slot = start + lax.broadcasted_iota(jnp.int32, (count, rows), 0)
        return (slot == place).astype(jnp.bfloat16)

    for load in loads[2:]:
        load.wait()
    e_one = exponent_of(one_in[...])
    code_one = encode(one_in[...], e_one)
    e_two = exponent_of(two_in[...])
    code_two = encode(two_in[...], e_two)
    for k, code in enumerate((code_one, code_two)):
        codes[:, (2 * k) * 256 : (2 * k + 1) * 256] = (code >> 8).astype(jnp.float32).astype(jnp.bfloat16)
        codes[:, (2 * k + 1) * 256 : (2 * k + 2) * 256] = (code & 255).astype(jnp.float32).astype(jnp.bfloat16)
    place_code = jnp.round(within_period(m_in[...]) * (1.0 / STEP)).astype(jnp.int32) & 0xFFFFF
    for k, code in enumerate((place_code >> 12, (place_code >> 4) & 255, place_code & 15)):
        codes[:, (4 + k) * 256 : (5 + k) * 256] = code.astype(jnp.float32).astype(jnp.bfloat16)
    tile = 256
    scales = ((e_one.astype(jnp.int32) + OFFSET) << 24) | ((e_two.astype(jnp.int32) + OFFSET) << 16)
    for j in range(1024 // tile):
        packed = jnp.dot(onehot(place_m, j * tile, tile), codes[...], preferred_element_type=jnp.float32)
        q = [packed[:, k * 256 : (k + 1) * 256] for k in range(7)]
        here = pl.ds(j * 8, 8)
        word = join((q[0] * 256.0 + q[1]).astype(jnp.int32), (q[2] * 256.0 + q[3]).astype(jnp.int32))
        psend[here, 0:32] = word.reshape(8, 32, 256)
        high = (q[4] * 256.0 + q[5]).astype(jnp.int32).reshape(8, 32, 256)
        psend[here, 32:48] = join(high[:, 0:16], high[:, 16:32])
        low = q[6].astype(jnp.int32).reshape(8, 4, 8, 256)
        low = low[:, 0] | (low[:, 1] << 4) | (low[:, 2] << 8) | (low[:, 3] << 12)
        psend[here, 48:56] = low | scales[None]

    def p_start(r, carry):
        p_copy(r).start()
        return carry

    p_self = pltpu.make_async_copy(psend.at[me], pout_ref.at[me], local_sem.at[6])
    p_self.start()

    service(1, 0)
    loads[0].wait()
    transpose_into(act_own, core * tokens)
    act_copy.wait_recv()
    transpose_into(act_sib, (1 - core) * tokens)

    hits = jnp.sum((writer_ref[...] == me).astype(jnp.float32), axis=1, keepdims=True)
    counts = jnp.broadcast_to(hits, (DP, 128)).astype(jnp.bfloat16)
    lower = lax.broadcasted_iota(jnp.int32, (DP + 8, DP), 0) > lax.broadcasted_iota(jnp.int32, (DP + 8, DP), 1)
    base_ref[...] = jnp.dot(lower.astype(jnp.bfloat16), counts, preferred_element_type=jnp.float32).astype(jnp.int32)

    def write_code(values, *refs):
        exponent = exponent_of(values)
        code = encode(values, exponent)
        word = join(code[0:words], code[words:rows])
        count = words // len(refs)
        for i, ref in enumerate(refs):
            ref[0:count] = word[i * count : (i + 1) * count]
            ref[count : count + SCALE_ROWS] = jnp.broadcast_to(
                exponent.astype(jnp.int32), (SCALE_ROWS, values.shape[1])
            )

    def add_code(ref, total, start, count):
        unit = unit_of(ref[count : count + 1, :].astype(jnp.float32))
        word = ref[0:count]
        total[start : start + count] += high_of(word).astype(jnp.float32) * unit
        total[words + start : words + start + count] += low_of(word).astype(jnp.float32) * unit

    def far_copy(slot, i):
        return remote(
            osend.at[slot, i], orecv.at[slot, i], os_sem.at[slot, i], or_sem.at[slot, i], left if i else right, plane
        )

    def near_copy(slot, i):
        return remote(
            nsend.at[slot, i], nrecv.at[slot, i], ns_sem.at[slot, i], nr_sem.at[slot, i], left if i else right, plane
        )

    def b_copy(slot):
        k = lax.rem(across - pair_of(slot) + SIDE, SIDE) - 1
        j = 0 if slot < 4 else 1
        return remote(
            bsend.at[slot], brecv.at[j, k], bs_sem.at[slot], br_sem.at[j, k], device(along, pair_of(slot)), plane
        )

    def multiply(slot):
        for o in range(2):
            block = jnp.dot(
                act_t[o * rows : (o + 1) * rows, :], cot_all[slot], preferred_element_type=jnp.float32
            )
            product[slot, 2 * o] = block[:, 0:128]
            product[slot, 2 * o + 1] = block[:, 128:256]
        write_code(product[slot, lax.rem(along + 2, SIDE)], osend.at[slot, 0], osend.at[slot, 1])
        far_copy(slot, 0).start()
        far_copy(slot, 1).start()

    def pass_on(slot):
        for i, turn in ((0, 1), (1, SIDE - 1)):
            target = lax.rem(along + turn, SIDE)
            far_copy(slot, i).wait_recv()
            add_code(orecv.at[slot, i], product.at[slot, target], i * (words // 2), words // 2)
            write_code(product[slot, target], nsend.at[slot, i])
            near_copy(slot, i).start()

    def reduce(slot):
        for i in range(2):
            near_copy(slot, i).wait_recv()
            add_code(nrecv.at[slot, i], product.at[slot, along], 0, words)

        @pl.when(across != pair_of(slot))
        def _():
            write_code(product[slot, along], bsend.at[slot])
            b_copy(slot).start()

    def p_move(j):
        return remote(
            zsend.at[j], zrecv.at[j], ps_sem.at[j], pr_sem.at[j], me, lax.rem(plane + shifts[j], PLANES)
        )

    def whole(j):
        slot = shifts[j]
        for k in range(SIDE - 1):
            source = lax.rem(across + k + 1, SIDE)
            remote(
                bsend.at[0], brecv.at[j, k], bs_sem.at[0], br_sem.at[j, k], device(along, source), plane
            ).wait_recv()
            add_code(brecv.at[j, k], product.at[slot, along], 0, words)
        write_code(product[slot, along], zsend.at[j])

    loads[1].wait()
    f_wait(0)
    multiply(0)
    for chunk in range(1, CHUNKS):
        service(1, chunk)
    for step in (1, 2, 3):
        f_wait(ORDER[step][0])
        multiply(ORDER[step][0])
        service(step + 1, 0)
        f_wait(ORDER[step][1])
        multiply(ORDER[step][1])
        service(step + 1, 1)
        for slot in ORDER[step - 1]:
            pass_on(slot)
        service(step + 1, 2)
        if step >= 2:
            for slot in ORDER[step - 2]:
                reduce(slot)
        service(step + 1, 3)
    f_wait(4)
    multiply(4)
    for slot in ORDER[3]:
        pass_on(slot)
    for slot in ORDER[2]:
        reduce(slot)
    pass_on(4)
    for slot in ORDER[3] + ORDER[4]:
        reduce(slot)

    whole(0)

    @pl.when(across != 0)
    def _():
        p_move(0).start()

    whole(1)
    p_move(1).start()
    lax.fori_loop(23, DP, p_start, 0)

    owners = [4 * lax.rem(plane + PLANES - shift, PLANES) + 2 * core + along // 2 for shift in shifts]
    for j in range(2):
        place_g = place_of(owners[j], True)
        if j == 0:

            @pl.when(across != 0)
            def _():
                p_move(0).wait_recv()

            @pl.when(across == 0)
            def _():
                zrecv[0] = zsend[0]

        else:
            p_move(1).wait_recv()
        exponent = zrecv[j, words : words + SCALE_ROWS]
        word = zrecv[j, 0:words]
        for k, code in enumerate((high_of(word), low_of(word))):
            codes[k * words : (k + 1) * words, 0:128] = (code >> 8).astype(jnp.float32).astype(jnp.bfloat16)
            codes[k * words : (k + 1) * words, 128:256] = (code & 255).astype(jnp.float32).astype(jnp.bfloat16)
        for i in range(2):
            q = []
            for side_of in range(2):
                packed = jnp.dot(
                    onehot(place_g, side_of * 512 + i * 256, 256), codes[:, 0:256], preferred_element_type=jnp.float32
                )
                q.append((packed[:, 0:128] * 256.0 + packed[:, 128:256]).astype(jnp.int32))
            gsend[i * 16 : (i + 1) * 16, j * 16 : (j + 1) * 16] = join(q[0], q[1]).reshape(16, 16, 128)
        gsend[:, 32 + 4 * j : 36 + 4 * j] = jnp.broadcast_to(exponent[None, 0:4], (DP, 4, 128))

    def g_copy(r):
        to = lax.rem(me + r, DP)
        return remote(gsend.at[to], gout_ref.at[me], gs_sem.at[r], gr_sem.at[r], to, plane)

    def g_start(r, carry):
        g_copy(r).start()
        return carry

    lax.fori_loop(1, DP, g_start, 0)
    g_self = pltpu.make_async_copy(gsend.at[me], gout_ref.at[me], local_sem.at[7])
    g_self.start()

    act_copy.wait_send()
    for slot in (0, 1, 2, 3, 5, 6, 7):
        for chunk in range(CHUNKS):
            if slot in (0, 1, 2):
                z_copy(slot, chunk, -1).wait_send()
            if slot in (0, 7, 6):
                z_copy(slot, chunk, 1).wait_send()
    for chunk in range(CHUNKS):
        z_last(chunk).wait_send()
    for slot in range(PLANES):
        for chunk in range(CHUNKS):
            f_copy(slot, chunk).wait_send()
        for i in range(2):
            far_copy(slot, i).wait_send()
            near_copy(slot, i).wait_send()

        @pl.when(across != pair_of(slot))
        def _():
            b_copy(slot).wait_send()

    @pl.when(across != 0)
    def _():
        p_move(0).wait_send()

    p_move(1).wait_send()
    p_self.wait()
    g_self.wait()

    def finish(r, carry):
        source = lax.rem(me + DP - r, DP)
        p_copy(r).wait_send()
        g_copy(r).wait_send()
        remote(psend.at[0], pout_ref.at[source], qs_sem.at[r], qr_sem.at[r], source, plane).wait_recv()
        remote(gsend.at[0], gout_ref.at[source], gs_sem.at[r], gr_sem.at[r], source, plane).wait_recv()
        return carry

    lax.fori_loop(1, DP, finish, 0)


def main_call(activations, cotangent, master, moment_one, moment_two, writers):
    tokens, features = activations.shape
    rows, width = master.shape
    half = features // CORES
    side = width // 2
    coded = (rows // 2 + SCALE_ROWS, side)
    any_space = pl.BlockSpec(memory_space=pl.ANY)
    vmem = pl.BlockSpec(memory_space=pltpu.VMEM)
    dma = pltpu.SemaphoreType.DMA
    f32, i32, bf16 = jnp.float32, jnp.int32, jnp.bfloat16
    return pl.pallas_call(
        main_kernel,
        name="reduce_and_regroup",
        out_shape=(
            jax.ShapeDtypeStruct((DP, 40, side), i32),
            jax.ShapeDtypeStruct((DP, 56, width), i32),
            jax.ShapeDtypeStruct((DP + 8, 128), i32),
        ),
        in_specs=[any_space] * 5 + [vmem],
        out_specs=(any_space, any_space, vmem),
        scratch_shapes=[
            pltpu.VMEM((tokens, half), bf16),
            pltpu.VMEM((tokens, half), bf16),
            pltpu.VMEM((half, 2 * tokens), bf16),
            pltpu.VMEM((PLANES, 2 * tokens, width), bf16),
            pltpu.VMEM((PLANES, SIDE, rows, side), f32),
            pltpu.VMEM((PLANES, 2, rows // 4 + SCALE_ROWS, side), i32),
            pltpu.VMEM((PLANES, 2, rows // 4 + SCALE_ROWS, side), i32),
            pltpu.VMEM((PLANES, 2) + coded, i32),
            pltpu.VMEM((PLANES, 2) + coded, i32),
            pltpu.VMEM((PLANES,) + coded, i32),
            pltpu.VMEM((2, SIDE - 1) + coded, i32),
            pltpu.VMEM((2,) + coded, i32),
            pltpu.VMEM((2,) + coded, i32),
            pltpu.VMEM((DP, 40, side), i32),
            pltpu.VMEM((rows, width), f32),
            pltpu.VMEM((rows, width), f32),
            pltpu.VMEM((rows, width), f32),
            pltpu.VMEM((DP, 56, width), i32),
            pltpu.VMEM((rows, 7 * width), bf16),
            pltpu.VMEM((DP, rows), i32),
            dma((8,)),
            dma((2,)),
            dma((1,)),
            dma((PLANES, CHUNKS)),
            dma((PLANES, CHUNKS)),
            dma((PLANES, CHUNKS)),
            dma((PLANES, CHUNKS)),
            dma((PLANES, 2)),
            dma((PLANES, 2)),
            dma((PLANES, 2)),
            dma((PLANES, 2)),
            dma((PLANES,)),
            dma((2, SIDE - 1)),
            dma((2,)),
            dma((2,)),
            dma((DP,)),
            dma((DP,)),
            dma((DP,)),
            dma((DP,)),
        ],
        compiler_params=pltpu.CompilerParams(
            collective_id=0, has_side_effects=True, vmem_limit_bytes=56 * 1024 * 1024
        ),
        cost_estimate=pl.CostEstimate(
            flops=4 * tokens * features * width * PLANES // 2, bytes_accessed=8 * 1024 * 1024, transcendentals=0
        ),
    )(activations, cotangent, master, moment_one, moment_two, writers)


def source_of(owner, part, plane):
    slot = lax.rem(plane + PLANES - owner // 4, PLANES)
    late = slot // 4
    across = jnp.where(late == 0, slot, lax.rem(PLANES - slot, 4))
    core = (owner // 2) % 2
    x, y = axes_of(2 * (owner % 2) + part, across, core)
    return (x * SIDE + y) * CORES + core, late


def finish_kernel(
    base_ref, gradient_hbm, moments_hbm, previous_hbm,
    delta_hbm, high_hbm, first_hbm, second_hbm,
    gradient_ref, moments_ref, previous_ref, rows_ref, delta_ref, high_ref, first_ref, second_ref, sem,
):
    groups = sem.shape[1]
    count = DP // groups
    capacity, width = previous_ref.shape
    block_rows = capacity // groups

    def group_loads(i):
        some = pl.ds(i * count, count)
        here = pl.ds(i * block_rows, block_rows)
        return [
            pltpu.make_async_copy(moments_hbm.at[some], moments_ref.at[some], sem.at[0, i]),
            pltpu.make_async_copy(previous_hbm.at[here], previous_ref.at[here], sem.at[2, i]),
        ]

    def group_stores(i):
        here = pl.ds(i * block_rows, block_rows)
        pairs = ((delta_ref, delta_hbm), (high_ref, high_hbm), (first_ref, first_hbm), (second_ref, second_hbm))
        return [
            pltpu.make_async_copy(ref.at[here], hbm.at[here], sem.at[3 + k, i]) for k, (ref, hbm) in enumerate(pairs)
        ]

    gradient_load = pltpu.make_async_copy(gradient_hbm, gradient_ref, sem.at[7, 0])
    gradient_load.start()
    for i in range(groups):
        for load in group_loads(i)[:1]:
            load.start()
    for i in range(groups):
        group_loads(i)[1].start()
    plane = lax.axis_index("tensor")
    pair = capacity // DP
    row = lax.broadcasted_iota(jnp.int32, (8, 3 * width), 0)
    gradient_load.wait()
    for owner in range(DP):
        if owner % count == 0:
            for load in group_loads(owner // count)[:1]:
                load.wait()
        parts = []
        for part in range(2):
            source, late = source_of(owner, part, plane)
            start = pl.multiple_of(late * 16, 8)
            exponent = gradient_ref[source, 32:40, :]
            exponent = jnp.where(late == 0, exponent[0:1], exponent[4:5])
            word = gradient_ref[source, pl.ds(start, 16), :]
            code = jnp.concatenate([high_of(word), low_of(word)], axis=0).astype(jnp.float32)
            parts.append(code * unit_of(exponent.astype(jnp.float32)))
        gradient = jnp.concatenate(parts, axis=1)
        word = moments_ref[owner, 0:32, :]
        tail = moments_ref[owner, 48:56, :]
        unit_one = unit_of((((tail[0:1] >> 24) & 255) - OFFSET).astype(jnp.float32))
        unit_two = unit_of((((tail[0:1] >> 16) & 255) - OFFSET).astype(jnp.float32))
        one = high_of(word).astype(jnp.float32) * unit_one
        two = low_of(word).astype(jnp.float32) * unit_two
        first, second = moments_of(gradient, one, two)
        word = moments_ref[owner, 32:48, :]
        low = jnp.concatenate([(tail >> (4 * t)) & 15 for t in range(4)], axis=0)
        code = (jnp.concatenate([(word >> 16) & 0xFFFF, word & 0xFFFF], axis=0) << 4) | low
        block = jnp.concatenate([code.astype(jnp.float32), first, second], axis=1)
        start = base_ref[owner, 0]
        offset = lax.rem(start, 8)
        aligned = pl.multiple_of(start - offset, 8)
        block = pltpu.roll(block, offset, 0)
        head = rows_ref.at[pl.ds(aligned, 8), :]
        head[...] = jnp.where(row >= offset, block[0:8], head[...])
        rows_ref[pl.ds(pl.multiple_of(aligned + 8, 8), pair - 8), :] = block[8:pair]
        rows_ref[pl.ds(pl.multiple_of(aligned + pair, 8), 8), :] = block[0:8]
    total = base_ref[DP, 0]
    for i in range(groups):
        group_loads(i)[1].wait()
        here = pl.ds(i * block_rows, block_rows)
        filled = i * block_rows + lax.broadcasted_iota(jnp.int32, (block_rows, width), 0) < total
        first = rows_ref[here, width : 2 * width]
        second = rows_ref[here, 2 * width : 3 * width]
        previous = previous_ref[here, :]
        ahead = rows_ref[here, 0:width] * STEP - within_period(previous)
        ahead = ahead - PERIOD * jnp.round(ahead * (1.0 / PERIOD))
        delta = jnp.where(filled, ahead / learn_rate - step_of(first, second, previous + ahead), 0.0)
        delta_ref[here, :] = delta
        high_ref[here, :] = delta.astype(jnp.bfloat16)
        first_ref[here, :] = jnp.where(filled, first, 0.0)
        second_ref[here, :] = jnp.where(filled, second, 0.0)
        for store in group_stores(i):
            store.start()
    for i in range(groups):
        for store in group_stores(i):
            store.wait()


def finish_call(base, gradient, moments, previous):
    capacity, width = previous.shape
    any_space = pl.BlockSpec(memory_space=pl.ANY)
    return pl.pallas_call(
        finish_kernel,
        name="update_and_place",
        out_shape=(
            jax.ShapeDtypeStruct((capacity, width), jnp.float32),
            jax.ShapeDtypeStruct((capacity, width), jnp.bfloat16),
            jax.ShapeDtypeStruct((capacity, width), jnp.float32),
            jax.ShapeDtypeStruct((capacity, width), jnp.float32),
        ),
        in_specs=[pl.BlockSpec(memory_space=pltpu.SMEM)] + [any_space] * 3,
        out_specs=(any_space,) * 4,
        scratch_shapes=[
            pltpu.VMEM(gradient.shape, gradient.dtype),
            pltpu.VMEM(moments.shape, moments.dtype),
            pltpu.VMEM(previous.shape, previous.dtype),
            pltpu.VMEM((capacity + capacity // DP + 8, 3 * width), jnp.float32),
            pltpu.VMEM((capacity, width), jnp.float32),
            pltpu.VMEM((capacity, width), jnp.bfloat16),
            pltpu.VMEM((capacity, width), jnp.float32),
            pltpu.VMEM((capacity, width), jnp.float32),
            pltpu.SemaphoreType.DMA((8, 4)),
        ],
        compiler_params=pltpu.CompilerParams(vmem_limit_bytes=60 * 1024 * 1024),
    )(base, gradient, moments, previous)


def local(activations, cotangent, master, moment_one, moment_two, writer_of, previous):
    writers = writer_of.reshape(-1, 128)
    gradient, moments, base = main_call(activations, cotangent, master, moment_one, moment_two, writers)
    return finish_call(base, gradient, moments, previous)


def solution(mesh):
    spec = P("dp", "tensor")
    return jax.shard_map(
        local,
        mesh=mesh,
        in_specs=(spec, spec, spec, spec, spec, P(), spec),
        out_specs=(spec, spec, spec, spec),
        check_vma=False,
    )
```

```python
import functools

import jax
import jax.numpy as jnp
from jax import lax
from jax.experimental import pallas as pl
from jax.experimental.pallas import tpu as pltpu
from jax.sharding import PartitionSpec as P

learn_rate = 0.01
beta_one = 0.9
beta_two = 0.95
epsilon = 1e-08
decay_rate = 0.1
bias_one = 1.0 - 0.9**10
bias_two = 1.0 - 0.95**10

MESH = pl.DeviceIdType.MESH
SIDE = 4
CORES = 2
DP = SIDE * SIDE * CORES
PLANES = 8
CHUNKS = 4
SCALE_ROWS = 8
TOP = 14.99
PERIOD = 0.625
STEP = PERIOD / 2**20
OFFSET = 128
SPREAD = ((1, 6), (6, 11), (11, 15), (15, 19), (19, 21), (21, 23), (23, 23), (23, 23), (23, 23), (23, 23), (23, 23), (23, 23), (23, 23), (23, 23), (23, 23), (23, 23))
ORDER = ((0,), (1, 7), (2, 6), (3, 5), (4,))


def moments_of(gradient, moment_one, moment_two):
    first = beta_one * moment_one + (1.0 - beta_one) * gradient
    second = beta_two * moment_two + (1.0 - beta_two) * gradient * gradient
    return first, second


def step_of(first, second, master):
    return first / bias_one / (jnp.sqrt(second / bias_two) + epsilon) + decay_rate * master


def exponent_of(values):
    most = jnp.max(jnp.abs(values), axis=0, keepdims=True)
    return jnp.ceil(jnp.log2(jnp.maximum(most, 1e-30)))


def encode(values, exponent):
    return jnp.round(values * jnp.exp2(TOP - exponent)).astype(jnp.int32)


def unit_of(exponent):
    return 1.0 / jnp.exp2(TOP - exponent)


def within_period(values):
    return values - jnp.floor(values * (1.0 / PERIOD)) * PERIOD


def join(high, low):
    return (high << 16) | (low & 0xFFFF)


def high_of(word):
    return word >> 16


def low_of(word):
    return (word << 16) >> 16


def coordinates():
    index = lax.axis_index("dp")
    return index // (SIDE * CORES), (index // CORES) % SIDE, index % CORES, lax.axis_index("tensor")


def axes_of(x, y, core):
    return x * (1 - core) + y * core, y * (1 - core) + x * core


def pair_of(slot):
    return slot if slot < 4 else (8 - slot) % 4


def shifts_of(across):
    return across, 8 - across - 4 * (1 - jnp.minimum(across, 1))


def main_kernel(
    act_ref, cot_ref, master_ref, one_ref, two_ref, writer_flat,
    gout_ref, pout_ref, base_ref,
    act_own, act_sib, act_t, cot_all, product, osend, orecv, nsend, nrecv, bsend, brecv, zsend, zrecv, gsend,
    m_in, one_in, two_in, psend, codes, writer_ref,
    local_sem, act_sem, cot_sib_sem, zs_sem, zr_sem, fs_sem, fr_sem, os_sem, or_sem, ns_sem, nr_sem, bs_sem, br_sem,
    ps_sem, pr_sem, gs_sem, gr_sem, qs_sem, qr_sem,
):
    x, y, core, plane = coordinates()
    me = lax.axis_index("dp")
    tokens, _ = cot_ref.shape
    half = act_own.shape[1]
    rows = master_ref.shape[0]
    words = rows // 2
    along, across = axes_of(x, y, core)
    shifts = shifts_of(across)
    sibling = me + 1 - 2 * core
    up = lax.rem(plane + 1, PLANES)
    down = lax.rem(plane + PLANES - 1, PLANES)
    part = tokens // CHUNKS

    def device(a, b):
        return ((a * (1 - core) + b * core) * SIDE + b * (1 - core) + a * core) * CORES + core

    right = device(lax.rem(along + 1, SIDE), across)
    left = device(lax.rem(along + SIDE - 1, SIDE), across)

    def remote(src, dst, send, recv, dp, at):
        return pltpu.make_async_remote_copy(
            src_ref=src, dst_ref=dst, send_sem=send, recv_sem=recv, device_id=(dp, at), device_id_type=MESH
        )

    def columns_of(which):
        return pl.ds(pl.multiple_of(which * half, 128), half)

    def own_rows(chunk=None):
        if chunk is None:
            return pl.ds(pl.multiple_of(core * tokens, 128), tokens)
        return pl.ds(pl.multiple_of(core * tokens + chunk * part, 64), part)

    loads = [
        pltpu.make_async_copy(act_ref.at[:, columns_of(core)], act_own, local_sem.at[0]),
        pltpu.make_async_copy(cot_ref, cot_all.at[0, own_rows()], local_sem.at[1]),
        pltpu.make_async_copy(master_ref, m_in, local_sem.at[2]),
        pltpu.make_async_copy(one_ref, one_in, local_sem.at[3]),
        pltpu.make_async_copy(two_ref, two_in, local_sem.at[4]),
    ]
    for load in loads:
        load.start()

    barrier = pltpu.get_barrier_semaphore()

    def greet(r, carry):
        pl.semaphore_signal(barrier, inc=1, device_id=(lax.rem(me + r, DP), plane), device_id_type=MESH)
        return carry

    lax.fori_loop(1, DP, greet, 0)
    for at in (up, down):
        pl.semaphore_signal(barrier, inc=1, device_id=(me, at), device_id_type=MESH)

    pl.semaphore_signal(
        barrier, inc=1, device_id=(me, lax.rem(plane + PLANES - shifts[1], PLANES)), device_id_type=MESH
    )

    @pl.when(across != 0)
    def _():
        pl.semaphore_signal(
            barrier, inc=1, device_id=(me, lax.rem(plane + PLANES - across, PLANES)), device_id_type=MESH
        )

    def place_of(owner, split):
        writers = writer_ref[pl.ds(owner, 1), :]
        mine = lax.broadcasted_iota(jnp.int32, (DP, rows), 0) == writers
        below = lax.broadcasted_iota(jnp.int32, (rows, rows), 0) < lax.broadcasted_iota(jnp.int32, (rows, rows), 1)
        before = jnp.dot(
            mine.astype(jnp.bfloat16), below.astype(jnp.bfloat16), preferred_element_type=jnp.float32
        )
        rank = jnp.sum(jnp.where(mine, before, 0.0), axis=0, keepdims=True).astype(jnp.int32)
        if split:
            return (rank >> 4) * (DP * 16) + writers * 16 + (rank & 15)
        return writers * 32 + rank

    for k in range(rows // 128):
        writer_ref[:, k * 128 : (k + 1) * 128] = writer_flat[pl.ds(k, DP, stride=rows // 128), :]

    place_m = place_of(me, False)
    pl.semaphore_wait(barrier, DP + 2 + jnp.minimum(across, 1))

    def z_copy(slot, chunk, direction):
        target = (slot - direction) % PLANES
        rows_here = pl.ds(pl.multiple_of(core * tokens + chunk * part, 64), part)
        if slot == 0:
            src = cot_ref.at[pl.ds(chunk * part, part)]
        else:
            src = cot_all.at[slot, rows_here]
        sem = (target, chunk)
        return remote(
            src, cot_all.at[target, rows_here], zs_sem.at[sem], zr_sem.at[sem], me, up if direction == 1 else down
        )

    def z_last(chunk):
        rows_here = pl.ds(pl.multiple_of(core * tokens + chunk * part, 64), part)
        return remote(
            cot_all.at[5 - 2 * core, rows_here], cot_all.at[4, rows_here], zs_sem.at[4, chunk], zr_sem.at[4, chunk],
            me, lax.rem(plane + 1 - 2 * core + PLANES, PLANES),
        )

    def f_copy(slot, chunk):
        rows_here = own_rows(chunk)
        src = cot_ref.at[pl.ds(chunk * part, part)] if slot == 0 else cot_all.at[slot, rows_here]
        sem = (slot, chunk)
        return remote(src, cot_all.at[slot, rows_here], fs_sem.at[sem], fr_sem.at[sem], sibling, plane)

    def f_wait(slot):
        for chunk in range(CHUNKS):
            other = pl.ds(pl.multiple_of((1 - core) * tokens + chunk * part, 64), part)
            sem = (slot, chunk)
            remote(
                cot_ref.at[pl.ds(0, part)], cot_all.at[slot, other], fs_sem.at[sem], fr_sem.at[sem], sibling, plane
            ).wait_recv()

    act_copy = remote(act_ref.at[:, columns_of(1 - core)], act_sib, act_sem.at[0], act_sem.at[1], sibling, plane)
    for chunk in range(CHUNKS):
        z_copy(0, chunk, 1).start()
        z_copy(0, chunk, -1).start()
    act_copy.start()
    for chunk in range(CHUNKS):
        f_copy(0, chunk).start()

    def z_wait(slot, chunk):
        rows_here = pl.ds(pl.multiple_of(core * tokens + chunk * part, 64), part)
        remote(
            cot_ref.at[pl.ds(0, part)], cot_all.at[slot, rows_here], zs_sem.at[slot, chunk], zr_sem.at[slot, chunk],
            me, up,
        ).wait_recv()

    def p_copy(r):
        to = lax.rem(me + r, DP)
        return remote(psend.at[to], pout_ref.at[me], qs_sem.at[r], qr_sem.at[r], to, plane)

    def service(step, chunk):
        for slot in ORDER[step]:
            z_wait(slot, chunk)
        if step < 3:
            z_copy(ORDER[step][1], chunk, 1).start()
            z_copy(ORDER[step][0], chunk, -1).start()
        elif step == 3:
            z_last(chunk).start()
        for slot in ORDER[step]:
            f_copy(slot, chunk).start()
        for r in range(*SPREAD[4 * step - 4 + chunk]):
            p_copy(r).start()

    def transpose_into(source, offset):
        for j in range(half // 128):
            act_t[j * 128 : (j + 1) * 128, pl.ds(pl.multiple_of(offset, 128), tokens)] = source[
                :, j * 128 : (j + 1) * 128
            ].T

    def onehot(place, start, count):
        slot = start + lax.broadcasted_iota(jnp.int32, (count, rows), 0)
        return (slot == place).astype(jnp.bfloat16)

    for load in loads[2:]:
        load.wait()
    e_one = exponent_of(one_in[...])
    code_one = encode(one_in[...], e_one)
    e_two = exponent_of(two_in[...])
    code_two = encode(two_in[...], e_two)
    for k, code in enumerate((code_one, code_two)):
        codes[:, (2 * k) * 256 : (2 * k + 1) * 256] = (code >> 8).astype(jnp.float32).astype(jnp.bfloat16)
        codes[:, (2 * k + 1) * 256 : (2 * k + 2) * 256] = (code & 255).astype(jnp.float32).astype(jnp.bfloat16)
    place_code = jnp.round(within_period(m_in[...]) * (1.0 / STEP)).astype(jnp.int32) & 0xFFFFF
    for k, code in enumerate((place_code >> 12, (place_code >> 4) & 255, place_code & 15)):
        codes[:, (4 + k) * 256 : (5 + k) * 256] = code.astype(jnp.float32).astype(jnp.bfloat16)
    tile = 256
    scales = ((e_one.astype(jnp.int32) + OFFSET) << 24) | ((e_two.astype(jnp.int32) + OFFSET) << 16)
    for j in range(1024 // tile):
        packed = jnp.dot(onehot(place_m, j * tile, tile), codes[...], preferred_element_type=jnp.float32)
        q = [packed[:, k * 256 : (k + 1) * 256] for k in range(7)]
        here = pl.ds(j * 8, 8)
        word = join((q[0] * 256.0 + q[1]).astype(jnp.int32), (q[2] * 256.0 + q[3]).astype(jnp.int32))
        psend[here, 0:32] = word.reshape(8, 32, 256)
        high = (q[4] * 256.0 + q[5]).astype(jnp.int32).reshape(8, 32, 256)
        psend[here, 32:48] = join(high[:, 0:16], high[:, 16:32])
        low = q[6].astype(jnp.int32).reshape(8, 4, 8, 256)
        low = low[:, 0] | (low[:, 1] << 4) | (low[:, 2] << 8) | (low[:, 3] << 12)
        psend[here, 48:56] = low | scales[None]

    def p_start(r, carry):
        p_copy(r).start()
        return carry

    p_self = pltpu.make_async_copy(psend.at[me], pout_ref.at[me], local_sem.at[6])
    p_self.start()

    service(1, 0)
    loads[0].wait()
    transpose_into(act_own, core * tokens)
    act_copy.wait_recv()
    transpose_into(act_sib, (1 - core) * tokens)

    hits = jnp.sum((writer_ref[...] == me).astype(jnp.float32), axis=1, keepdims=True)
    counts = jnp.broadcast_to(hits, (DP, 128)).astype(jnp.bfloat16)
    lower = lax.broadcasted_iota(jnp.int32, (DP + 8, DP), 0) > lax.broadcasted_iota(jnp.int32, (DP + 8, DP), 1)
    base_ref[...] = jnp.dot(lower.astype(jnp.bfloat16), counts, preferred_element_type=jnp.float32).astype(jnp.int32)

    def write_code(values, *refs):
        exponent = exponent_of(values)
        code = encode(values, exponent)
        word = join(code[0:words], code[words:rows])
        count = words // len(refs)
        for i, ref in enumerate(refs):
            ref[0:count] = word[i * count : (i + 1) * count]
            ref[count : count + SCALE_ROWS] = jnp.broadcast_to(
                exponent.astype(jnp.int32), (SCALE_ROWS, values.shape[1])
            )

    def add_code(ref, total, start, count):
        unit = unit_of(ref[count : count + 1, :].astype(jnp.float32))
        word = ref[0:count]
        total[start : start + count] += high_of(word).astype(jnp.float32) * unit
        total[words + start : words + start + count] += low_of(word).astype(jnp.float32) * unit

    def far_copy(slot, i):
        return remote(
            osend.at[slot, i], orecv.at[slot, i], os_sem.at[slot, i], or_sem.at[slot, i], left if i else right, plane
        )

    def near_copy(slot, i):
        return remote(
            nsend.at[slot, i], nrecv.at[slot, i], ns_sem.at[slot, i], nr_sem.at[slot, i], left if i else right, plane
        )

    def b_copy(slot):
        k = lax.rem(across - pair_of(slot) + SIDE, SIDE) - 1
        j = 0 if slot < 4 else 1
        return remote(
            bsend.at[slot], brecv.at[j, k], bs_sem.at[slot], br_sem.at[j, k], device(along, pair_of(slot)), plane
        )

    def multiply(slot):
        for o in range(2):
            block = jnp.dot(
                act_t[o * rows : (o + 1) * rows, :], cot_all[slot], preferred_element_type=jnp.float32
            )
            product[slot, 2 * o] = block[:, 0:128]
            product[slot, 2 * o + 1] = block[:, 128:256]
        write_code(product[slot, lax.rem(along + 2, SIDE)], osend.at[slot, 0], osend.at[slot, 1])
        far_copy(slot, 0).start()
        far_copy(slot, 1).start()

    def pass_on(slot):
        for i, turn in ((0, 1), (1, SIDE - 1)):
            target = lax.rem(along + turn, SIDE)
            far_copy(slot, i).wait_recv()
            add_code(orecv.at[slot, i], product.at[slot, target], i * (words // 2), words // 2)
            write_code(product[slot, target], nsend.at[slot, i])
            near_copy(slot, i).start()

    def reduce(slot):
        for i in range(2):
            near_copy(slot, i).wait_recv()
            add_code(nrecv.at[slot, i], product.at[slot, along], 0, words)

        @pl.when(across != pair_of(slot))
        def _():
            write_code(product[slot, along], bsend.at[slot])
            b_copy(slot).start()

    def p_move(j):
        return remote(
            zsend.at[j], zrecv.at[j], ps_sem.at[j], pr_sem.at[j], me, lax.rem(plane + shifts[j], PLANES)
        )

    def whole(j):
        slot = shifts[j]
        for k in range(SIDE - 1):
            source = lax.rem(across + k + 1, SIDE)
            remote(
                bsend.at[0], brecv.at[j, k], bs_sem.at[0], br_sem.at[j, k], device(along, source), plane
            ).wait_recv()
            add_code(brecv.at[j, k], product.at[slot, along], 0, words)
        write_code(product[slot, along], zsend.at[j])

    loads[1].wait()
    f_wait(0)
    multiply(0)
    for chunk in range(1, CHUNKS):
        service(1, chunk)
    for step in (1, 2, 3):
        f_wait(ORDER[step][0])
        multiply(ORDER[step][0])
        service(step + 1, 0)
        f_wait(ORDER[step][1])
        multiply(ORDER[step][1])
        service(step + 1, 1)
        for slot in ORDER[step - 1]:
            pass_on(slot)
        service(step + 1, 2)
        if step >= 2:
            for slot in ORDER[step - 2]:
                reduce(slot)
        service(step + 1, 3)
    f_wait(4)
    multiply(4)
    for slot in ORDER[3]:
        pass_on(slot)
    for slot in ORDER[2]:
        reduce(slot)
    pass_on(4)
    for slot in ORDER[3] + ORDER[4]:
        reduce(slot)

    whole(0)

    @pl.when(across != 0)
    def _():
        p_move(0).start()

    whole(1)
    p_move(1).start()
    lax.fori_loop(23, DP, p_start, 0)

    owners = [4 * lax.rem(plane + PLANES - shift, PLANES) + 2 * core + along // 2 for shift in shifts]
    for j in range(2):
        place_g = place_of(owners[j], True)
        if j == 0:

            @pl.when(across != 0)
            def _():
                p_move(0).wait_recv()

            @pl.when(across == 0)
            def _():
                zrecv[0] = zsend[0]

        else:
            p_move(1).wait_recv()
        exponent = zrecv[j, words : words + SCALE_ROWS]
        word = zrecv[j, 0:words]
        for k, code in enumerate((high_of(word), low_of(word))):
            codes[k * words : (k + 1) * words, 0:128] = (code >> 8).astype(jnp.float32).astype(jnp.bfloat16)
            codes[k * words : (k + 1) * words, 128:256] = (code & 255).astype(jnp.float32).astype(jnp.bfloat16)
        for i in range(2):
            q = []
            for side_of in range(2):
                packed = jnp.dot(
                    onehot(place_g, side_of * 512 + i * 256, 256), codes[:, 0:256], preferred_element_type=jnp.float32
                )
                q.append((packed[:, 0:128] * 256.0 + packed[:, 128:256]).astype(jnp.int32))
            gsend[i * 16 : (i + 1) * 16, j * 16 : (j + 1) * 16] = join(q[0], q[1]).reshape(16, 16, 128)
        gsend[:, 32 + 4 * j : 36 + 4 * j] = jnp.broadcast_to(exponent[None, 0:4], (DP, 4, 128))

    def g_copy(r):
        to = lax.rem(me + r, DP)
        return remote(gsend.at[to], gout_ref.at[me], gs_sem.at[r], gr_sem.at[r], to, plane)

    def g_start(r, carry):
        g_copy(r).start()
        return carry

    lax.fori_loop(1, DP, g_start, 0)
    g_self = pltpu.make_async_copy(gsend.at[me], gout_ref.at[me], local_sem.at[7])
    g_self.start()

    act_copy.wait_send()
    for slot in (0, 1, 2, 3, 5, 6, 7):
        for chunk in range(CHUNKS):
            if slot in (0, 1, 2):
                z_copy(slot, chunk, -1).wait_send()
            if slot in (0, 7, 6):
                z_copy(slot, chunk, 1).wait_send()
    for chunk in range(CHUNKS):
        z_last(chunk).wait_send()
    for slot in range(PLANES):
        for chunk in range(CHUNKS):
            f_copy(slot, chunk).wait_send()
        for i in range(2):
            far_copy(slot, i).wait_send()
            near_copy(slot, i).wait_send()

        @pl.when(across != pair_of(slot))
        def _():
            b_copy(slot).wait_send()

    @pl.when(across != 0)
    def _():
        p_move(0).wait_send()

    p_move(1).wait_send()
    p_self.wait()
    g_self.wait()

    def finish(r, carry):
        source = lax.rem(me + DP - r, DP)
        p_copy(r).wait_send()
        g_copy(r).wait_send()
        remote(psend.at[0], pout_ref.at[source], qs_sem.at[r], qr_sem.at[r], source, plane).wait_recv()
        remote(gsend.at[0], gout_ref.at[source], gs_sem.at[r], gr_sem.at[r], source, plane).wait_recv()
        return carry

    lax.fori_loop(1, DP, finish, 0)


def main_call(activations, cotangent, master, moment_one, moment_two, writers):
    tokens, features = activations.shape
    rows, width = master.shape
    half = features // CORES
    side = width // 2
    coded = (rows // 2 + SCALE_ROWS, side)
    any_space = pl.BlockSpec(memory_space=pl.ANY)
    vmem = pl.BlockSpec(memory_space=pltpu.VMEM)
    dma = pltpu.SemaphoreType.DMA
    f32, i32, bf16 = jnp.float32, jnp.int32, jnp.bfloat16
    return pl.pallas_call(
        main_kernel,
        name="reduce_and_regroup",
        out_shape=(
            jax.ShapeDtypeStruct((DP, 40, side), i32),
            jax.ShapeDtypeStruct((DP, 56, width), i32),
            jax.ShapeDtypeStruct((DP + 8, 128), i32),
        ),
        in_specs=[any_space] * 5 + [vmem],
        out_specs=(any_space, any_space, vmem),
        scratch_shapes=[
            pltpu.VMEM((tokens, half), bf16),
            pltpu.VMEM((tokens, half), bf16),
            pltpu.VMEM((half, 2 * tokens), bf16),
            pltpu.VMEM((PLANES, 2 * tokens, width), bf16),
            pltpu.VMEM((PLANES, SIDE, rows, side), f32),
            pltpu.VMEM((PLANES, 2, rows // 4 + SCALE_ROWS, side), i32),
            pltpu.VMEM((PLANES, 2, rows // 4 + SCALE_ROWS, side), i32),
            pltpu.VMEM((PLANES, 2) + coded, i32),
            pltpu.VMEM((PLANES, 2) + coded, i32),
            pltpu.VMEM((PLANES,) + coded, i32),
            pltpu.VMEM((2, SIDE - 1) + coded, i32),
            pltpu.VMEM((2,) + coded, i32),
            pltpu.VMEM((2,) + coded, i32),
            pltpu.VMEM((DP, 40, side), i32),
            pltpu.VMEM((rows, width), f32),
            pltpu.VMEM((rows, width), f32),
            pltpu.VMEM((rows, width), f32),
            pltpu.VMEM((DP, 56, width), i32),
            pltpu.VMEM((rows, 7 * width), bf16),
            pltpu.VMEM((DP, rows), i32),
            dma((8,)),
            dma((2,)),
            dma((1,)),
            dma((PLANES, CHUNKS)),
            dma((PLANES, CHUNKS)),
            dma((PLANES, CHUNKS)),
            dma((PLANES, CHUNKS)),
            dma((PLANES, 2)),
            dma((PLANES, 2)),
            dma((PLANES, 2)),
            dma((PLANES, 2)),
            dma((PLANES,)),
            dma((2, SIDE - 1)),
            dma((2,)),
            dma((2,)),
            dma((DP,)),
            dma((DP,)),
            dma((DP,)),
            dma((DP,)),
        ],
        compiler_params=pltpu.CompilerParams(
            collective_id=0, has_side_effects=True, vmem_limit_bytes=56 * 1024 * 1024
        ),
        cost_estimate=pl.CostEstimate(
            flops=4 * tokens * features * width * PLANES // 2, bytes_accessed=8 * 1024 * 1024, transcendentals=0
        ),
    )(activations, cotangent, master, moment_one, moment_two, writers)


def source_of(owner, part, plane):
    slot = lax.rem(plane + PLANES - owner // 4, PLANES)
    late = slot // 4
    across = jnp.where(late == 0, slot, lax.rem(PLANES - slot, 4))
    core = (owner // 2) % 2
    x, y = axes_of(2 * (owner % 2) + part, across, core)
    return (x * SIDE + y) * CORES + core, late


def finish_kernel(
    base_ref, gradient_hbm, moments_hbm, previous_hbm,
    delta_hbm, high_hbm, first_hbm, second_hbm,
    gradient_ref, moments_ref, previous_ref, rows_ref, delta_ref, high_ref, first_ref, second_ref, sem,
):
    groups = sem.shape[1]
    count = DP // groups
    capacity, width = previous_ref.shape
    block_rows = capacity // groups

    def group_loads(i):
        some = pl.ds(i * count, count)
        here = pl.ds(i * block_rows, block_rows)
        return [
            pltpu.make_async_copy(moments_hbm.at[some], moments_ref.at[some], sem.at[0, i]),
            pltpu.make_async_copy(previous_hbm.at[here], previous_ref.at[here], sem.at[2, i]),
        ]

    def group_stores(i):
        here = pl.ds(i * block_rows, block_rows)
        pairs = ((delta_ref, delta_hbm), (high_ref, high_hbm), (first_ref, first_hbm), (second_ref, second_hbm))
        return [
            pltpu.make_async_copy(ref.at[here], hbm.at[here], sem.at[3 + k, i]) for k, (ref, hbm) in enumerate(pairs)
        ]

    gradient_load = pltpu.make_async_copy(gradient_hbm, gradient_ref, sem.at[7, 0])
    gradient_load.start()
    for i in range(groups):
        for load in group_loads(i)[:1]:
            load.start()
    for i in range(groups):
        group_loads(i)[1].start()
    plane = lax.axis_index("tensor")
    pair = capacity // DP
    row = lax.broadcasted_iota(jnp.int32, (8, 3 * width), 0)
    gradient_load.wait()
    for owner in range(DP):
        if owner % count == 0:
            for load in group_loads(owner // count)[:1]:
                load.wait()
        parts = []
        for part in range(2):
            source, late = source_of(owner, part, plane)
            start = pl.multiple_of(late * 16, 8)
            exponent = gradient_ref[source, 32:40, :]
            exponent = jnp.where(late == 0, exponent[0:1], exponent[4:5])
            word = gradient_ref[source, pl.ds(start, 16), :]
            code = jnp.concatenate([high_of(word), low_of(word)], axis=0).astype(jnp.float32)
            parts.append(code * unit_of(exponent.astype(jnp.float32)))
        gradient = jnp.concatenate(parts, axis=1)
        word = moments_ref[owner, 0:32, :]
        tail = moments_ref[owner, 48:56, :]
        unit_one = unit_of((((tail[0:1] >> 24) & 255) - OFFSET).astype(jnp.float32))
        unit_two = unit_of((((tail[0:1] >> 16) & 255) - OFFSET).astype(jnp.float32))
        one = high_of(word).astype(jnp.float32) * unit_one
        two = low_of(word).astype(jnp.float32) * unit_two
        first, second = moments_of(gradient, one, two)
        word = moments_ref[owner, 32:48, :]
        low = jnp.concatenate([(tail >> (4 * t)) & 15 for t in range(4)], axis=0)
        code = (jnp.concatenate([(word >> 16) & 0xFFFF, word & 0xFFFF], axis=0) << 4) | low
        block = jnp.concatenate([code.astype(jnp.float32), first, second], axis=1)
        start = base_ref[owner, 0]
        offset = lax.rem(start, 8)
        aligned = pl.multiple_of(start - offset, 8)
        block = pltpu.roll(block, offset, 0)
        head = rows_ref.at[pl.ds(aligned, 8), :]
        head[...] = jnp.where(row >= offset, block[0:8], head[...])
        rows_ref[pl.ds(pl.multiple_of(aligned + 8, 8), pair - 8), :] = block[8:pair]
        rows_ref[pl.ds(pl.multiple_of(aligned + pair, 8), 8), :] = block[0:8]
    total = base_ref[DP, 0]
    for i in range(groups):
        group_loads(i)[1].wait()
        here = pl.ds(i * block_rows, block_rows)
        filled = i * block_rows + lax.broadcasted_iota(jnp.int32, (block_rows, width), 0) < total
        first = rows_ref[here, width : 2 * width]
        second = rows_ref[here, 2 * width : 3 * width]
        previous = previous_ref[here, :]
        ahead = rows_ref[here, 0:width] * STEP - within_period(previous)
        ahead = ahead - PERIOD * jnp.round(ahead * (1.0 / PERIOD))
        delta = jnp.where(filled, ahead / learn_rate - step_of(first, second, previous + ahead), 0.0)
        delta_ref[here, :] = delta
        high_ref[here, :] = delta.astype(jnp.bfloat16)
        first_ref[here, :] = jnp.where(filled, first, 0.0)
        second_ref[here, :] = jnp.where(filled, second, 0.0)
        for store in group_stores(i):
            store.start()
    for i in range(groups):
        for store in group_stores(i):
            store.wait()


def finish_call(base, gradient, moments, previous):
    capacity, width = previous.shape
    any_space = pl.BlockSpec(memory_space=pl.ANY)
    return pl.pallas_call(
        finish_kernel,
        name="update_and_place",
        out_shape=(
            jax.ShapeDtypeStruct((capacity, width), jnp.float32),
            jax.ShapeDtypeStruct((capacity, width), jnp.bfloat16),
            jax.ShapeDtypeStruct((capacity, width), jnp.float32),
            jax.ShapeDtypeStruct((capacity, width), jnp.float32),
        ),
        in_specs=[pl.BlockSpec(memory_space=pltpu.SMEM)] + [any_space] * 3,
        out_specs=(any_space,) * 4,
        scratch_shapes=[
            pltpu.VMEM(gradient.shape, gradient.dtype),
            pltpu.VMEM(moments.shape, moments.dtype),
            pltpu.VMEM(previous.shape, previous.dtype),
            pltpu.VMEM((capacity + capacity // DP + 8, 3 * width), jnp.float32),
            pltpu.VMEM((capacity, width), jnp.float32),
            pltpu.VMEM((capacity, width), jnp.bfloat16),
            pltpu.VMEM((capacity, width), jnp.float32),
            pltpu.VMEM((capacity, width), jnp.float32),
            pltpu.SemaphoreType.DMA((8, 4)),
        ],
        compiler_params=pltpu.CompilerParams(vmem_limit_bytes=60 * 1024 * 1024),
    )(base, gradient, moments, previous)


def local(activations, cotangent, master, moment_one, moment_two, writer_of, previous):
    writers = writer_of.reshape(-1, 128)
    gradient, moments, base = main_call(activations, cotangent, master, moment_one, moment_two, writers)
    return finish_call(base, gradient, moments, previous)


def solution(mesh):
    spec = P("dp", "tensor")
    return jax.shard_map(
        local,
        mesh=mesh,
        in_specs=(spec, spec, spec, spec, spec, P(), spec),
        out_specs=(spec, spec, spec, spec),
        check_vma=False,
    )
```

```python
import functools

import jax
import jax.numpy as jnp
from jax import lax
from jax.experimental import pallas as pl
from jax.experimental.pallas import tpu as pltpu
from jax.sharding import PartitionSpec as P

learn_rate = 0.01
beta_one = 0.9
beta_two = 0.95
epsilon = 1e-08
decay_rate = 0.1
bias_one = 1.0 - 0.9**10
bias_two = 1.0 - 0.95**10

MESH = pl.DeviceIdType.MESH
SIDE = 4
CORES = 2
DP = SIDE * SIDE * CORES
PLANES = 8
CHUNKS = 4
SCALE_ROWS = 8
TOP = 14.99
PERIOD = 0.625
STEP = PERIOD / 2**20
OFFSET = 128
SPREAD = ((1, 6), (6, 11), (11, 15), (15, 19), (19, 21), (21, 23), (23, 23), (23, 23), (23, 23), (23, 23), (23, 23), (23, 23), (23, 23), (23, 23), (23, 23), (23, 23))
ORDER = ((0,), (1, 7), (2, 6), (3, 5), (4,))


def moments_of(gradient, moment_one, moment_two):
    first = beta_one * moment_one + (1.0 - beta_one) * gradient
    second = beta_two * moment_two + (1.0 - beta_two) * gradient * gradient
    return first, second


def step_of(first, second, master):
    return first / bias_one / (jnp.sqrt(second / bias_two) + epsilon) + decay_rate * master


def exponent_of(values):
    most = jnp.max(jnp.abs(values), axis=0, keepdims=True)
    return jnp.ceil(jnp.log2(jnp.maximum(most, 1e-30)))


def encode(values, exponent):
    return jnp.round(values * jnp.exp2(TOP - exponent)).astype(jnp.int32)


def unit_of(exponent):
    return 1.0 / jnp.exp2(TOP - exponent)


def within_period(values):
    return values - jnp.floor(values * (1.0 / PERIOD)) * PERIOD


def join(high, low):
    return (high << 16) | (low & 0xFFFF)


def high_of(word):
    return word >> 16


def low_of(word):
    return (word << 16) >> 16


def coordinates():
    index = lax.axis_index("dp")
    return index // (SIDE * CORES), (index // CORES) % SIDE, index % CORES, lax.axis_index("tensor")


def axes_of(x, y, core):
    return x * (1 - core) + y * core, y * (1 - core) + x * core


def pair_of(slot):
    return slot if slot < 4 else (8 - slot) % 4


def shifts_of(across):
    return across, 8 - across - 4 * (1 - jnp.minimum(across, 1))


def main_kernel(
    act_ref, cot_ref, master_ref, one_ref, two_ref, writer_flat,
    gout_ref, pout_ref, base_ref,
    act_own, act_sib, act_t, cot_all, product, osend, orecv, nsend, nrecv, bsend, brecv, zsend, zrecv, gsend,
    m_in, one_in, two_in, psend, codes, writer_ref,
    local_sem, act_sem, cot_sib_sem, zs_sem, zr_sem, fs_sem, fr_sem, os_sem, or_sem, ns_sem, nr_sem, bs_sem, br_sem,
    ps_sem, pr_sem, gs_sem, gr_sem, qs_sem, qr_sem,
):
    x, y, core, plane = coordinates()
    me = lax.axis_index("dp")
    tokens, _ = cot_ref.shape
    half = act_own.shape[1]
    rows = master_ref.shape[0]
    words = rows // 2
    along, across = axes_of(x, y, core)
    shifts = shifts_of(across)
    sibling = me + 1 - 2 * core
    up = lax.rem(plane + 1, PLANES)
    down = lax.rem(plane + PLANES - 1, PLANES)
    part = tokens // CHUNKS

    def device(a, b):
        return ((a * (1 - core) + b * core) * SIDE + b * (1 - core) + a * core) * CORES + core

    right = device(lax.rem(along + 1, SIDE), across)
    left = device(lax.rem(along + SIDE - 1, SIDE), across)

    def remote(src, dst, send, recv, dp, at):
        return pltpu.make_async_remote_copy(
            src_ref=src, dst_ref=dst, send_sem=send, recv_sem=recv, device_id=(dp, at), device_id_type=MESH
        )

    def columns_of(which):
        return pl.ds(pl.multiple_of(which * half, 128), half)

    def own_rows(chunk=None):
        if chunk is None:
            return pl.ds(pl.multiple_of(core * tokens, 128), tokens)
        return pl.ds(pl.multiple_of(core * tokens + chunk * part, 64), part)

    loads = [
        pltpu.make_async_copy(act_ref.at[:, columns_of(core)], act_own, local_sem.at[0]),
        pltpu.make_async_copy(cot_ref, cot_all.at[0, own_rows()], local_sem.at[1]),
        pltpu.make_async_copy(master_ref, m_in, local_sem.at[2]),
        pltpu.make_async_copy(one_ref, one_in, local_sem.at[3]),
        pltpu.make_async_copy(two_ref, two_in, local_sem.at[4]),
    ]
    for load in loads:
        load.start()

    barrier = pltpu.get_barrier_semaphore()

    def greet(r, carry):
        pl.semaphore_signal(barrier, inc=1, device_id=(lax.rem(me + r, DP), plane), device_id_type=MESH)
        return carry

    lax.fori_loop(1, DP, greet, 0)
    for at in (up, down):
        pl.semaphore_signal(barrier, inc=1, device_id=(me, at), device_id_type=MESH)

    pl.semaphore_signal(
        barrier, inc=1, device_id=(me, lax.rem(plane + PLANES - shifts[1], PLANES)), device_id_type=MESH
    )

    @pl.when(across != 0)
    def _():
        pl.semaphore_signal(
            barrier, inc=1, device_id=(me, lax.rem(plane + PLANES - across, PLANES)), device_id_type=MESH
        )

    def place_of(owner, split):
        writers = writer_ref[pl.ds(owner, 1), :]
        mine = lax.broadcasted_iota(jnp.int32, (DP, rows), 0) == writers
        below = lax.broadcasted_iota(jnp.int32, (rows, rows), 0) < lax.broadcasted_iota(jnp.int32, (rows, rows), 1)
        before = jnp.dot(
            mine.astype(jnp.bfloat16), below.astype(jnp.bfloat16), preferred_element_type=jnp.float32
        )
        rank = jnp.sum(jnp.where(mine, before, 0.0), axis=0, keepdims=True).astype(jnp.int32)
        if split:
            return (rank >> 4) * (DP * 16) + writers * 16 + (rank & 15)
        return writers * 32 + rank

    for k in range(rows // 128):
        writer_ref[:, k * 128 : (k + 1) * 128] = writer_flat[pl.ds(k, DP, stride=rows // 128), :]

    place_m = place_of(me, False)
    pl.semaphore_wait(barrier, DP + 2 + jnp.minimum(across, 1))

    def z_copy(slot, chunk, direction):
        target = (slot - direction) % PLANES
        rows_here = pl.ds(pl.multiple_of(core * tokens + chunk * part, 64), part)
        if slot == 0:
            src = cot_ref.at[pl.ds(chunk * part, part)]
        else:
            src = cot_all.at[slot, rows_here]
        sem = (target, chunk)
        return remote(
            src, cot_all.at[target, rows_here], zs_sem.at[sem], zr_sem.at[sem], me, up if direction == 1 else down
        )

    def z_last(chunk):
        rows_here = pl.ds(pl.multiple_of(core * tokens + chunk * part, 64), part)
        return remote(
            cot_all.at[5 - 2 * core, rows_here], cot_all.at[4, rows_here], zs_sem.at[4, chunk], zr_sem.at[4, chunk],
            me, lax.rem(plane + 1 - 2 * core + PLANES, PLANES),
        )

    def f_copy(slot, chunk):
        rows_here = own_rows(chunk)
        src = cot_ref.at[pl.ds(chunk * part, part)] if slot == 0 else cot_all.at[slot, rows_here]
        sem = (slot, chunk)
        return remote(src, cot_all.at[slot, rows_here], fs_sem.at[sem], fr_sem.at[sem], sibling, plane)

    def f_wait(slot):
        for chunk in range(CHUNKS):
            other = pl.ds(pl.multiple_of((1 - core) * tokens + chunk * part, 64), part)
            sem = (slot, chunk)
            remote(
                cot_ref.at[pl.ds(0, part)], cot_all.at[slot, other], fs_sem.at[sem], fr_sem.at[sem], sibling, plane
            ).wait_recv()

    act_copy = remote(act_ref.at[:, columns_of(1 - core)], act_sib, act_sem.at[0], act_sem.at[1], sibling, plane)
    for chunk in range(CHUNKS):
        z_copy(0, chunk, 1).start()
        z_copy(0, chunk, -1).start()
    act_copy.start()
    for chunk in range(CHUNKS):
        f_copy(0, chunk).start()

    def z_wait(slot, chunk):
        rows_here = pl.ds(pl.multiple_of(core * tokens + chunk * part, 64), part)
        remote(
            cot_ref.at[pl.ds(0, part)], cot_all.at[slot, rows_here], zs_sem.at[slot, chunk], zr_sem.at[slot, chunk],
            me, up,
        ).wait_recv()

    def p_copy(r):
        to = lax.rem(me + r, DP)
        return remote(psend.at[to], pout_ref.at[me], qs_sem.at[r], qr_sem.at[r], to, plane)

    def service(step, chunk):
        for slot in ORDER[step]:
            z_wait(slot, chunk)
        if step < 3:
            z_copy(ORDER[step][1], chunk, 1).start()
            z_copy(ORDER[step][0], chunk, -1).start()
        elif step == 3:
            z_last(chunk).start()
        for slot in ORDER[step]:
            f_copy(slot, chunk).start()
        for r in range(*SPREAD[4 * step - 4 + chunk]):
            p_copy(r).start()

    def transpose_into(source, offset):
        for j in range(half // 128):
            act_t[j * 128 : (j + 1) * 128, pl.ds(pl.multiple_of(offset, 128), tokens)] = source[
                :, j * 128 : (j + 1) * 128
            ].T

    def onehot(place, start, count):
        slot = start + lax.broadcasted_iota(jnp.int32, (count, rows), 0)
        return (slot == place).astype(jnp.bfloat16)

    for load in loads[2:]:
        load.wait()
    e_one = exponent_of(one_in[...])
    code_one = encode(one_in[...], e_one)
    e_two = exponent_of(two_in[...])
    code_two = encode(two_in[...], e_two)
    for k, code in enumerate((code_one, code_two)):
        codes[:, (2 * k) * 256 : (2 * k + 1) * 256] = (code >> 8).astype(jnp.float32).astype(jnp.bfloat16)
        codes[:, (2 * k + 1) * 256 : (2 * k + 2) * 256] = (code & 255).astype(jnp.float32).astype(jnp.bfloat16)
    place_code = jnp.round(within_period(m_in[...]) * (1.0 / STEP)).astype(jnp.int32) & 0xFFFFF
    for k, code in enumerate((place_code >> 12, (place_code >> 4) & 255, place_code & 15)):
        codes[:, (4 + k) * 256 : (5 + k) * 256] = code.astype(jnp.float32).astype(jnp.bfloat16)
    tile = 256
    scales = ((e_one.astype(jnp.int32) + OFFSET) << 24) | ((e_two.astype(jnp.int32) + OFFSET) << 16)
    for j in range(1024 // tile):
        packed = jnp.dot(onehot(place_m, j * tile, tile), codes[...], preferred_element_type=jnp.float32)
        q = [packed[:, k * 256 : (k + 1) * 256] for k in range(7)]
        here = pl.ds(j * 8, 8)
        word = join((q[0] * 256.0 + q[1]).astype(jnp.int32), (q[2] * 256.0 + q[3]).astype(jnp.int32))
        psend[here, 0:32] = word.reshape(8, 32, 256)
        high = (q[4] * 256.0 + q[5]).astype(jnp.int32).reshape(8, 32, 256)
        psend[here, 32:48] = join(high[:, 0:16], high[:, 16:32])
        low = q[6].astype(jnp.int32).reshape(8, 4, 8, 256)
        low = low[:, 0] | (low[:, 1] << 4) | (low[:, 2] << 8) | (low[:, 3] << 12)
        psend[here, 48:56] = low | scales[None]

    def p_start(r, carry):
        p_copy(r).start()
        return carry

    p_self = pltpu.make_async_copy(psend.at[me], pout_ref.at[me], local_sem.at[6])
    p_self.start()

    service(1, 0)
    loads[0].wait()
    transpose_into(act_own, core * tokens)
    act_copy.wait_recv()
    transpose_into(act_sib, (1 - core) * tokens)

    hits = jnp.sum((writer_ref[...] == me).astype(jnp.float32), axis=1, keepdims=True)
    counts = jnp.broadcast_to(hits, (DP, 128)).astype(jnp.bfloat16)
    lower = lax.broadcasted_iota(jnp.int32, (DP + 8, DP), 0) > lax.broadcasted_iota(jnp.int32, (DP + 8, DP), 1)
    base_ref[...] = jnp.dot(lower.astype(jnp.bfloat16), counts, preferred_element_type=jnp.float32).astype(jnp.int32)

    def write_code(values, *refs):
        exponent = exponent_of(values)
        code = encode(values, exponent)
        word = join(code[0:words], code[words:rows])
        count = words // len(refs)
        for i, ref in enumerate(refs):
            ref[0:count] = word[i * count : (i + 1) * count]
            ref[count : count + SCALE_ROWS] = jnp.broadcast_to(
                exponent.astype(jnp.int32), (SCALE_ROWS, values.shape[1])
            )

    def add_code(ref, total, start, count):
        unit = unit_of(ref[count : count + 1, :].astype(jnp.float32))
        word = ref[0:count]
        total[start : start + count] += high_of(word).astype(jnp.float32) * unit
        total[words + start : words + start + count] += low_of(word).astype(jnp.float32) * unit

    def far_copy(slot, i):
        return remote(
            osend.at[slot, i], orecv.at[slot, i], os_sem.at[slot, i], or_sem.at[slot, i], left if i else right, plane
        )

    def near_copy(slot, i):
        return remote(
            nsend.at[slot, i], nrecv.at[slot, i], ns_sem.at[slot, i], nr_sem.at[slot, i], left if i else right, plane
        )

    def b_copy(slot):
        k = lax.rem(across - pair_of(slot) + SIDE, SIDE) - 1
        j = 0 if slot < 4 else 1
        return remote(
            bsend.at[slot], brecv.at[j, k], bs_sem.at[slot], br_sem.at[j, k], device(along, pair_of(slot)), plane
        )

    def multiply(slot):
        for o in range(2):
            block = jnp.dot(
                act_t[o * rows : (o + 1) * rows, :], cot_all[slot], preferred_element_type=jnp.float32
            )
            product[slot, 2 * o] = block[:, 0:128]
            product[slot, 2 * o + 1] = block[:, 128:256]
        write_code(product[slot, lax.rem(along + 2, SIDE)], osend.at[slot, 0], osend.at[slot, 1])
        far_copy(slot, 0).start()
        far_copy(slot, 1).start()

    def pass_on(slot):
        for i, turn in ((0, 1), (1, SIDE - 1)):
            target = lax.rem(along + turn, SIDE)
            far_copy(slot, i).wait_recv()
            add_code(orecv.at[slot, i], product.at[slot, target], i * (words // 2), words // 2)
            write_code(product[slot, target], nsend.at[slot, i])
            near_copy(slot, i).start()

    def reduce(slot):
        for i in range(2):
            near_copy(slot, i).wait_recv()
            add_code(nrecv.at[slot, i], product.at[slot, along], 0, words)

        @pl.when(across != pair_of(slot))
        def _():
            write_code(product[slot, along], bsend.at[slot])
            b_copy(slot).start()

    def p_move(j):
        return remote(
            zsend.at[j], zrecv.at[j], ps_sem.at[j], pr_sem.at[j], me, lax.rem(plane + shifts[j], PLANES)
        )

    def whole(j):
        slot = shifts[j]
        for k in range(SIDE - 1):
            source = lax.rem(across + k + 1, SIDE)
            remote(
                bsend.at[0], brecv.at[j, k], bs_sem.at[0], br_sem.at[j, k], device(along, source), plane
            ).wait_recv()
            add_code(brecv.at[j, k], product.at[slot, along], 0, words)
        write_code(product[slot, along], zsend.at[j])

    loads[1].wait()
    f_wait(0)
    multiply(0)
    for chunk in range(1, CHUNKS):
        service(1, chunk)
    for step in (1, 2, 3):
        f_wait(ORDER[step][0])
        multiply(ORDER[step][0])
        service(step + 1, 0)
        f_wait(ORDER[step][1])
        multiply(ORDER[step][1])
        service(step + 1, 1)
        for slot in ORDER[step - 1]:
            pass_on(slot)
        service(step + 1, 2)
        if step >= 2:
            for slot in ORDER[step - 2]:
                reduce(slot)
        service(step + 1, 3)
    f_wait(4)
    multiply(4)
    for slot in ORDER[3]:
        pass_on(slot)
    for slot in ORDER[2]:
        reduce(slot)
    pass_on(4)
    for slot in ORDER[3] + ORDER[4]:
        reduce(slot)

    whole(0)

    @pl.when(across != 0)
    def _():
        p_move(0).start()

    whole(1)
    p_move(1).start()
    lax.fori_loop(23, DP, p_start, 0)

    owners = [4 * lax.rem(plane + PLANES - shift, PLANES) + 2 * core + along // 2 for shift in shifts]
    for j in range(2):
        place_g = place_of(owners[j], True)
        if j == 0:

            @pl.when(across != 0)
            def _():
                p_move(0).wait_recv()

            @pl.when(across == 0)
            def _():
                zrecv[0] = zsend[0]

        else:
            p_move(1).wait_recv()
        exponent = zrecv[j, words : words + SCALE_ROWS]
        word = zrecv[j, 0:words]
        for k, code in enumerate((high_of(word), low_of(word))):
            codes[k * words : (k + 1) * words, 0:128] = (code >> 8).astype(jnp.float32).astype(jnp.bfloat16)
            codes[k * words : (k + 1) * words, 128:256] = (code & 255).astype(jnp.float32).astype(jnp.bfloat16)
        for i in range(2):
            q = []
            for side_of in range(2):
                packed = jnp.dot(
                    onehot(place_g, side_of * 512 + i * 256, 256), codes[:, 0:256], preferred_element_type=jnp.float32
                )
                q.append((packed[:, 0:128] * 256.0 + packed[:, 128:256]).astype(jnp.int32))
            gsend[i * 16 : (i + 1) * 16, j * 16 : (j + 1) * 16] = join(q[0], q[1]).reshape(16, 16, 128)
        gsend[:, 32 + 4 * j : 36 + 4 * j] = jnp.broadcast_to(exponent[None, 0:4], (DP, 4, 128))

    def g_copy(r):
        to = lax.rem(me + r, DP)
        return remote(gsend.at[to], gout_ref.at[me], gs_sem.at[r], gr_sem.at[r], to, plane)

    def g_start(r, carry):
        g_copy(r).start()
        return carry

    lax.fori_loop(1, DP, g_start, 0)
    g_self = pltpu.make_async_copy(gsend.at[me], gout_ref.at[me], local_sem.at[7])
    g_self.start()

    act_copy.wait_send()
    for slot in (0, 1, 2, 3, 5, 6, 7):
        for chunk in range(CHUNKS):
            if slot in (0, 1, 2):
                z_copy(slot, chunk, -1).wait_send()
            if slot in (0, 7, 6):
                z_copy(slot, chunk, 1).wait_send()
    for chunk in range(CHUNKS):
        z_last(chunk).wait_send()
    for slot in range(PLANES):
        for chunk in range(CHUNKS):
            f_copy(slot, chunk).wait_send()
        for i in range(2):
            far_copy(slot, i).wait_send()
            near_copy(slot, i).wait_send()

        @pl.when(across != pair_of(slot))
        def _():
            b_copy(slot).wait_send()

    @pl.when(across != 0)
    def _():
        p_move(0).wait_send()

    p_move(1).wait_send()
    p_self.wait()
    g_self.wait()

    def finish(r, carry):
        source = lax.rem(me + DP - r, DP)
        p_copy(r).wait_send()
        g_copy(r).wait_send()
        remote(psend.at[0], pout_ref.at[source], qs_sem.at[r], qr_sem.at[r], source, plane).wait_recv()
        return carry

    def arrive(r, carry):
        source = lax.rem(me + DP - r, DP)
        remote(gsend.at[0], gout_ref.at[source], gs_sem.at[r], gr_sem.at[r], source, plane).wait_recv()
        return carry

    lax.fori_loop(1, DP, finish, 0)
    lax.fori_loop(1, DP, arrive, 0)


def main_call(activations, cotangent, master, moment_one, moment_two, writers):
    tokens, features = activations.shape
    rows, width = master.shape
    half = features // CORES
    side = width // 2
    coded = (rows // 2 + SCALE_ROWS, side)
    any_space = pl.BlockSpec(memory_space=pl.ANY)
    vmem = pl.BlockSpec(memory_space=pltpu.VMEM)
    dma = pltpu.SemaphoreType.DMA
    f32, i32, bf16 = jnp.float32, jnp.int32, jnp.bfloat16
    return pl.pallas_call(
        main_kernel,
        name="reduce_and_regroup",
        out_shape=(
            jax.ShapeDtypeStruct((DP, 40, side), i32),
            jax.ShapeDtypeStruct((DP, 56, width), i32),
            jax.ShapeDtypeStruct((DP + 8, 128), i32),
        ),
        in_specs=[any_space] * 5 + [vmem],
        out_specs=(any_space, any_space, vmem),
        scratch_shapes=[
            pltpu.VMEM((tokens, half), bf16),
            pltpu.VMEM((tokens, half), bf16),
            pltpu.VMEM((half, 2 * tokens), bf16),
            pltpu.VMEM((PLANES, 2 * tokens, width), bf16),
            pltpu.VMEM((PLANES, SIDE, rows, side), f32),
            pltpu.VMEM((PLANES, 2, rows // 4 + SCALE_ROWS, side), i32),
            pltpu.VMEM((PLANES, 2, rows // 4 + SCALE_ROWS, side), i32),
            pltpu.VMEM((PLANES, 2) + coded, i32),
            pltpu.VMEM((PLANES, 2) + coded, i32),
            pltpu.VMEM((PLANES,) + coded, i32),
            pltpu.VMEM((2, SIDE - 1) + coded, i32),
            pltpu.VMEM((2,) + coded, i32),
            pltpu.VMEM((2,) + coded, i32),
            pltpu.VMEM((DP, 40, side), i32),
            pltpu.VMEM((rows, width), f32),
            pltpu.VMEM((rows, width), f32),
            pltpu.VMEM((rows, width), f32),
            pltpu.VMEM((DP, 56, width), i32),
            pltpu.VMEM((rows, 7 * width), bf16),
            pltpu.VMEM((DP, rows), i32),
            dma((8,)),
            dma((2,)),
            dma((1,)),
            dma((PLANES, CHUNKS)),
            dma((PLANES, CHUNKS)),
            dma((PLANES, CHUNKS)),
            dma((PLANES, CHUNKS)),
            dma((PLANES, 2)),
            dma((PLANES, 2)),
            dma((PLANES, 2)),
            dma((PLANES, 2)),
            dma((PLANES,)),
            dma((2, SIDE - 1)),
            dma((2,)),
            dma((2,)),
            dma((DP,)),
            dma((DP,)),
            dma((DP,)),
            dma((DP,)),
        ],
        compiler_params=pltpu.CompilerParams(
            collective_id=0, has_side_effects=True, vmem_limit_bytes=56 * 1024 * 1024
        ),
        cost_estimate=pl.CostEstimate(
            flops=4 * tokens * features * width * PLANES // 2, bytes_accessed=8 * 1024 * 1024, transcendentals=0
        ),
    )(activations, cotangent, master, moment_one, moment_two, writers)


def source_of(owner, part, plane):
    slot = lax.rem(plane + PLANES - owner // 4, PLANES)
    late = slot // 4
    across = jnp.where(late == 0, slot, lax.rem(PLANES - slot, 4))
    core = (owner // 2) % 2
    x, y = axes_of(2 * (owner % 2) + part, across, core)
    return (x * SIDE + y) * CORES + core, late


def finish_kernel(
    base_ref, gradient_hbm, moments_hbm, previous_hbm,
    delta_hbm, high_hbm, first_hbm, second_hbm,
    gradient_ref, moments_ref, previous_ref, rows_ref, delta_ref, high_ref, first_ref, second_ref, sem,
):
    groups = sem.shape[1]
    count = DP // groups
    capacity, width = previous_ref.shape
    block_rows = capacity // groups

    def group_loads(i):
        some = pl.ds(i * count, count)
        here = pl.ds(i * block_rows, block_rows)
        return [
            pltpu.make_async_copy(moments_hbm.at[some], moments_ref.at[some], sem.at[0, i]),
            pltpu.make_async_copy(previous_hbm.at[here], previous_ref.at[here], sem.at[2, i]),
        ]

    def group_stores(i):
        here = pl.ds(i * block_rows, block_rows)
        pairs = ((delta_ref, delta_hbm), (high_ref, high_hbm), (first_ref, first_hbm), (second_ref, second_hbm))
        return [
            pltpu.make_async_copy(ref.at[here], hbm.at[here], sem.at[3 + k, i]) for k, (ref, hbm) in enumerate(pairs)
        ]

    gradient_load = pltpu.make_async_copy(gradient_hbm, gradient_ref, sem.at[7, 0])
    gradient_load.start()
    for i in range(groups):
        for load in group_loads(i)[:1]:
            load.start()
    for i in range(groups):
        group_loads(i)[1].start()
    plane = lax.axis_index("tensor")
    pair = capacity // DP
    row = lax.broadcasted_iota(jnp.int32, (8, 3 * width), 0)
    gradient_load.wait()
    for owner in range(DP):
        if owner % count == 0:
            for load in group_loads(owner // count)[:1]:
                load.wait()
        parts = []
        for part in range(2):
            source, late = source_of(owner, part, plane)
            start = pl.multiple_of(late * 16, 8)
            exponent = gradient_ref[source, 32:40, :]
            exponent = jnp.where(late == 0, exponent[0:1], exponent[4:5])
            word = gradient_ref[source, pl.ds(start, 16), :]
            code = jnp.concatenate([high_of(word), low_of(word)], axis=0).astype(jnp.float32)
            parts.append(code * unit_of(exponent.astype(jnp.float32)))
        gradient = jnp.concatenate(parts, axis=1)
        word = moments_ref[owner, 0:32, :]
        tail = moments_ref[owner, 48:56, :]
        unit_one = unit_of((((tail[0:1] >> 24) & 255) - OFFSET).astype(jnp.float32))
        unit_two = unit_of((((tail[0:1] >> 16) & 255) - OFFSET).astype(jnp.float32))
        one = high_of(word).astype(jnp.float32) * unit_one
        two = low_of(word).astype(jnp.float32) * unit_two
        first, second = moments_of(gradient, one, two)
        word = moments_ref[owner, 32:48, :]
        low = jnp.concatenate([(tail >> (4 * t)) & 15 for t in range(4)], axis=0)
        code = (jnp.concatenate([(word >> 16) & 0xFFFF, word & 0xFFFF], axis=0) << 4) | low
        block = jnp.concatenate([code.astype(jnp.float32), first, second], axis=1)
        start = base_ref[owner, 0]
        offset = lax.rem(start, 8)
        aligned = pl.multiple_of(start - offset, 8)
        block = pltpu.roll(block, offset, 0)
        head = rows_ref.at[pl.ds(aligned, 8), :]
        head[...] = jnp.where(row >= offset, block[0:8], head[...])
        rows_ref[pl.ds(pl.multiple_of(aligned + 8, 8), pair - 8), :] = block[8:pair]
        rows_ref[pl.ds(pl.multiple_of(aligned + pair, 8), 8), :] = block[0:8]
    total = base_ref[DP, 0]
    for i in range(groups):
        group_loads(i)[1].wait()
        here = pl.ds(i * block_rows, block_rows)
        filled = i * block_rows + lax.broadcasted_iota(jnp.int32, (block_rows, width), 0) < total
        first = rows_ref[here, width : 2 * width]
        second = rows_ref[here, 2 * width : 3 * width]
        previous = previous_ref[here, :]
        ahead = rows_ref[here, 0:width] * STEP - within_period(previous)
        ahead = ahead - PERIOD * jnp.round(ahead * (1.0 / PERIOD))
        delta = jnp.where(filled, ahead / learn_rate - step_of(first, second, previous + ahead), 0.0)
        delta_ref[here, :] = delta
        high_ref[here, :] = delta.astype(jnp.bfloat16)
        first_ref[here, :] = jnp.where(filled, first, 0.0)
        second_ref[here, :] = jnp.where(filled, second, 0.0)
        for store in group_stores(i):
            store.start()
    for i in range(groups):
        for store in group_stores(i):
            store.wait()


def finish_call(base, gradient, moments, previous):
    capacity, width = previous.shape
    any_space = pl.BlockSpec(memory_space=pl.ANY)
    return pl.pallas_call(
        finish_kernel,
        name="update_and_place",
        out_shape=(
            jax.ShapeDtypeStruct((capacity, width), jnp.float32),
            jax.ShapeDtypeStruct((capacity, width), jnp.bfloat16),
            jax.ShapeDtypeStruct((capacity, width), jnp.float32),
            jax.ShapeDtypeStruct((capacity, width), jnp.float32),
        ),
        in_specs=[pl.BlockSpec(memory_space=pltpu.SMEM)] + [any_space] * 3,
        out_specs=(any_space,) * 4,
        scratch_shapes=[
            pltpu.VMEM(gradient.shape, gradient.dtype),
            pltpu.VMEM(moments.shape, moments.dtype),
            pltpu.VMEM(previous.shape, previous.dtype),
            pltpu.VMEM((capacity + capacity // DP + 8, 3 * width), jnp.float32),
            pltpu.VMEM((capacity, width), jnp.float32),
            pltpu.VMEM((capacity, width), jnp.bfloat16),
            pltpu.VMEM((capacity, width), jnp.float32),
            pltpu.VMEM((capacity, width), jnp.float32),
            pltpu.SemaphoreType.DMA((8, 4)),
        ],
        compiler_params=pltpu.CompilerParams(vmem_limit_bytes=60 * 1024 * 1024),
    )(base, gradient, moments, previous)


def local(activations, cotangent, master, moment_one, moment_two, writer_of, previous):
    writers = writer_of.reshape(-1, 128)
    gradient, moments, base = main_call(activations, cotangent, master, moment_one, moment_two, writers)
    return finish_call(base, gradient, moments, previous)


def solution(mesh):
    spec = P("dp", "tensor")
    return jax.shard_map(
        local,
        mesh=mesh,
        in_specs=(spec, spec, spec, spec, spec, P(), spec),
        out_specs=(spec, spec, spec, spec),
        check_vma=False,
    )
```
